512 devices in a mesh: pair: 4 (over x), src: 8 (over z), tgt: 16 (over y, core).
Axes of the slice: x: 4, y: 8, z: 8, core: 2. Of those that a mesh axis runs over, the one named last changes fastest.
Arguments:
- src_cells: float32 [4, 30, 4096], P('pair', None, 'src'), may hold values from -17 to 17
- final_cells: float32 [30, 4096], P(None, 'tgt'), may hold values from -17 to 17
- growth: float32 [4, 4096], P('pair', 'src'), may hold values from 0.5 to 2
- live: int32 [5], replicated, may hold values from 1024 to 4096, as said below
- final_fates: float32 [40, 4096], P(None, 'tgt'), may hold values from 0 to 1
Outputs:
- fate_maps: float32 [4, 40, 4096], P('pair', None, ('src', 'tgt'))
- potentials: float32 [4, 4096], P('pair', 'src')
The draws below stay inside these ranges and needn't reach their ends.
Inputs may be any that keep to these rules, and one draw needn't show every extreme that they name: `live`: every count is at least 1024 and one snapshot fills all 4096 slots.
All inputs are finite; a program needn't handle non-finite values.
Results may differ from the reference program's by a relative error of at most 0.0049.
Values may be sent and summed in bfloat16 or wider, within the bound.
A program may use at most 64 MiB of HBM per device.

```python
import math
import jax
import jax.numpy as jnp
from jax import lax

D = 30
FATES = 40
N = 4096
ITERS = 8
PAIRS = 4


def draw_live(key, part):
    first_key, second_key = jax.random.split(key)
    counts = jax.random.randint(first_key, (PAIRS + 1,), N // 4, N + 1)
    filled = jax.random.randint(second_key, (), 0, PAIRS + 1)
    return jnp.where(jnp.arange(PAIRS + 1) == filled, N, counts).astype(jnp.int32)


def atlas_tables(key):
    lineages = 32
    lineage_base = jax.random.uniform(jax.random.fold_in(key, 101), (lineages, D), jnp.float32, -3.0, 3.0)
    section_reach = jnp.exp(jax.random.uniform(jax.random.fold_in(key, 102), (lineages, 1), jnp.float32, math.log(1.5), math.log(4.5)))
    sign_table = jax.random.randint(jax.random.fold_in(key, 103), (lineages, D), 0, 2).astype(jnp.float32) * 2.0 - 1.0
    section_step = section_reach * sign_table / math.sqrt(D)
    centres = jnp.stack([lineage_base, lineage_base + section_step], axis=1).reshape(2 * lineages, D)
    fate_of = (jax.random.permutation(jax.random.fold_in(key, 104), 2 * lineages) % FATES).astype(jnp.int32)
    flip_signs = jax.random.randint(jax.random.fold_in(key, 105), (D,), 0, 2).astype(jnp.float32) * 2.0 - 1.0
    return (centres, fate_of, flip_signs)


def cell_states(key, snapshot):
    lineages = 32
    snap_key = jax.random.fold_in(jax.random.fold_in(key, 201), snapshot)
    lineage = jax.random.randint(jax.random.fold_in(snap_key, 1), (N,), 0, lineages)
    section_share = jax.random.randint(jax.random.fold_in(snap_key, 2), (lineages,), 15, 86)
    section_roll = jax.random.randint(jax.random.fold_in(snap_key, 3), (N,), 0, 100)
    section_bit = (section_roll < section_share[lineage]).astype(jnp.int32)
    return (2 * lineage + section_bit).astype(jnp.int32)


def place_cells(key, snapshot, jitter):
    centres, fate_of, flip_signs = atlas_tables(key)
    states = cell_states(key, snapshot)
    offset_side = 10.0 - 20.0 * (snapshot % 2)
    return offset_side * flip_signs[:, None] + centres[states].T + jitter


def draw_src_cells(key, part):
    jitter_key = jax.random.fold_in(key, 21)
    jitter = jnp.clip(jax.random.normal(jitter_key, (PAIRS, D, N), jnp.float32), -3.0, 3.0)
    return jnp.stack([place_cells(key, snapshot, jitter[snapshot]) for snapshot in range(PAIRS)])


def draw_final_cells(key, part):
    jitter_key = jax.random.fold_in(key, 31)
    jitter = jnp.clip(jax.random.normal(jitter_key, (D, N), jnp.float32), -3.0, 3.0)
    return place_cells(key, PAIRS, jitter)


def draw_final_fates(key, part):
    centres, fate_of, flip_signs = atlas_tables(key)
    states = cell_states(key, PAIRS)
    fate_ids = fate_of[states]
    marked = (jnp.arange(FATES, dtype=jnp.int32)[:, None] == fate_ids[None, :]).astype(jnp.float32)
    background = jax.random.uniform(jax.random.fold_in(key, 301), (FATES, N), jnp.float32, 0.0, 1.0)
    return 0.8 * marked + 0.2 * background


def levels(own_key, dims, cuts, least, high):
    factor_of, own = 1.0, jax.random.fold_in(own_key, 6)
    for position, parts in cuts:
        heights = jnp.exp(jax.random.uniform(jax.random.fold_in(own, position), (parts,), jnp.float32, least / len(cuts), high / len(cuts)))
        factor_of = factor_of * jnp.repeat(heights, dims[position] // parts).reshape([-1 if axis == position else 1 for axis in range(len(dims))])
    return factor_of


def setup_inputs(seed: int = 0) -> dict:
    key_list = jax.random.split(jax.random.key(seed), 6)
    src_cells = draw_src_cells(jax.random.fold_in(key_list[5], 71), 0)
    final_cells = draw_final_cells(jax.random.fold_in(key_list[5], 71), 0)
    growth = jnp.clip(jnp.exp(math.log(2.0) - 1.3862944 * jax.random.uniform(key_list[2], (PAIRS, N), jnp.float32) ** levels(key_list[2], (PAIRS, N), ((0, 4), (1, 8)), -0.2, 0.2)), 0.5, 2.0)
    live = draw_live(jax.random.fold_in(key_list[5], 71), 0)
    final_fates = draw_final_fates(jax.random.fold_in(key_list[5], 71), 0)
    return dict(src_cells=src_cells, final_cells=final_cells, growth=growth, live=live, final_fates=final_fates)


EPS = 0.1
LAM = 1.0
NEG = -1.0e30


def pair_cost(source_pos, target_pos):
    cross = lax.dot_general(source_pos, target_pos, (((0,), (0,)), ((), ())), precision=lax.Precision.HIGHEST, preferred_element_type=jnp.float32)
    src_sq = jnp.sum(source_pos * source_pos, axis=0)
    tgt_sq = jnp.sum(target_pos * target_pos, axis=0)
    return (src_sq[:, None] + tgt_sq[None, :] - 2.0 * cross) / (2.0 * source_pos.shape[0])


def reference(src_cells, final_cells, growth, live, final_fates):
    shrink = LAM / (LAM + EPS)
    pair_count = src_cells.shape[0]
    slots = src_cells.shape[2]
    positions = jnp.arange(slots, dtype=jnp.int32)
    handed = final_fates.astype(jnp.bfloat16)
    fate_list = [None] * pair_count
    pot_list = [None] * pair_count
    for pair_num in reversed(range(pair_count)):
        source_pos = src_cells[pair_num]
        target_pos = src_cells[pair_num + 1] if pair_num + 1 < pair_count else final_cells
        cost_tile = pair_cost(source_pos, target_pos)
        live_src = positions < live[pair_num]
        live_tgt = positions < live[pair_num + 1]
        log_mass_a = jnp.where(live_src, jnp.log(growth[pair_num]) - jnp.log(live[pair_num].astype(jnp.float32)), NEG)
        log_mass_b = jnp.where(live_tgt, -jnp.log(live[pair_num + 1].astype(jnp.float32)) * jnp.ones((slots,), jnp.float32), NEG)
        pot_src = jnp.zeros((slots,), jnp.float32)
        pot_tgt = jnp.zeros((slots,), jnp.float32)
        for step_num in range(ITERS):
            col_scores = (pot_src[:, None] - cost_tile) / EPS + log_mass_a[:, None]
            col_peak = jnp.max(col_scores, axis=0)
            col_total = jnp.sum(jnp.exp(col_scores - col_peak[None, :]), axis=0)
            pot_tgt = -shrink * EPS * (col_peak + jnp.log(col_total))
            row_scores = (pot_tgt[None, :] - cost_tile) / EPS + log_mass_b[None, :]
            row_peak = jnp.max(row_scores, axis=1)
            row_total = jnp.sum(jnp.exp(row_scores - row_peak[:, None]), axis=1)
            pot_src = -shrink * EPS * (row_peak + jnp.log(row_total))
        weights = (jnp.exp(row_scores - row_peak[:, None]) / row_total[:, None]).astype(jnp.bfloat16)
        pulled = lax.dot_general(handed, weights, (((1,), (1,)), ((), ())), preferred_element_type=jnp.float32)
        pulled = jnp.where(live_src[None, :], pulled, 0.0)
        fate_list[pair_num] = pulled
        pot_list[pair_num] = pot_src
        handed = pulled.astype(jnp.bfloat16)
    return jnp.stack(fate_list), jnp.stack(pot_list)
```

```python
import functools
import math

import jax
import jax.numpy as jnp
from jax import lax
from jax.experimental import pallas as pl
from jax.experimental.pallas import tpu as pltpu
from jax.sharding import PartitionSpec as P

MESH = pl.DeviceIdType.MESH
F32 = jnp.float32
BF16 = jnp.bfloat16

ITERS = 8
EPS = 0.1
LAM = 1.0
NEG = -1e30
SHRINK = LAM / (LAM + EPS)
LOG2E = 1.0 / math.log(2.0)
COST_SCALE = LOG2E / (EPS * 60.0)
LOWEST = -3e38

HALF = 2048
QUARTER = 1024
LANES = 128


def lane_iota():
    return lax.broadcasted_iota(jnp.int32, (8, LANES), 1)


def sub_iota():
    return lax.broadcasted_iota(jnp.int32, (8, LANES), 0)


def spread_columns(packed, dst, base):
    def body(k, carry):
        turned = pltpu.roll(packed, lax.rem(LANES - 32 * k, LANES), axis=1)
        for t in range(32):
            row = pl.multiple_of(base + (32 * k + t) * 8, 8)
            dst[pl.ds(row, 8), :] = jnp.broadcast_to(turned[:, t : t + 1], (8, LANES))
        return carry

    lax.fori_loop(0, LANES // 32, body, 0)


def lse_pass(cost, spread, rows, tiles, group):
    def walk(start, update):
        def body(k, acc):
            acc = list(acc)
            for t in range(group):
                row = pl.multiple_of((k * group + t) * 8, 8)
                left = spread[pl.ds(row, 8), :]
                for q in range(tiles):
                    acc[q] = update(q, acc[q], left - cost[pl.ds(row, 8), LANES * q : LANES * (q + 1)])
            return tuple(acc)

        return lax.fori_loop(0, rows // (8 * group), body, tuple(start))

    peaks = walk([jnp.full((8, LANES), LOWEST, F32)] * tiles, lambda q, a, s: jnp.maximum(a, s))
    peaks = [jnp.broadcast_to(jnp.max(a, axis=0, keepdims=True), (8, LANES)) for a in peaks]
    sums = walk([jnp.zeros((8, LANES), F32)] * tiles, lambda q, a, s: a + jnp.exp2(s - peaks[q]))
    sums = [jnp.broadcast_to(jnp.sum(a, axis=0, keepdims=True), (8, LANES)) for a in sums]
    which = sub_iota()
    out = []
    for r in range(tiles // 8):
        m, s = peaks[8 * r], sums[8 * r]
        for q in range(1, 8):
            m = jnp.where(which == q, peaks[8 * r + q], m)
            s = jnp.where(which == q, sums[8 * r + q], s)
        out.append((m, s))
    return out


def three_parts(x):
    high = x.astype(BF16).astype(F32)
    rest = x - high
    mid = rest.astype(BF16).astype(F32)
    low = (rest - mid).astype(BF16).astype(F32)
    return high, mid, low


def kernel(
    src_ref, fin_ref, growth_ref, live_ref, fates_ref, out_ref, pot_ref,
    xst, fst, fates_st, xbuf, ybuf, xk, xt0, xt1, yt, yts, ct, cr, ub, vb, wt,
    csend, cslot, rsend, rslot, fsend, fother, hand, pbuf, pbf, chin, s1, s2st, s2,
    in_send, x_sem, y_sem, f_sem, fs_send, cs_send, cs_recv, rs_send, rs_recv,
    p_send, p_recv, ch_send, ch_recv, s1_send, s1_recv, s2_send, s2_recv,
):
    p = lax.axis_index("pair")
    z = lax.axis_index("src")
    t = lax.axis_index("tgt")
    y, c = t // 2, t % 2
    zb, yb = z % 2, y % 2
    b = 2 * zb + yb
    z0, y0 = z - zb, y - yb
    a, d = z // 2, y // 2
    home = z // 4
    last = p == 3

    def at(pp, zz, yy, cc):
        return {"pair": pp, "src": zz, "tgt": 2 * yy + cc}

    def push(src, dst, send, recv, where):
        return pltpu.make_async_remote_copy(src, dst, send, recv, device_id=where, device_id_type=MESH)

    def same(pp, zz, yy, cc):
        return (pp == p) & (zz == z) & (yy == y) & (cc == c)

    up, down = jnp.minimum(p + 1, 3), jnp.maximum(p - 1, 0)
    chips = [((b + k) % 4) for k in range(1, 4)]
    chip_at = lambda bb: (z0 + bb // 2, y0 + bb % 2)
    core_peer = (p, z, y, 1 - c)
    row_peers = [(p, *chip_at(bb), c) for bb in chips]
    x_to = [(c == home, (p, (z + k) % 8, y, c)) for k in range(1, 8)]
    x_from = [(4 * c + k != z, (p, 4 * c + k, y, c)) for k in range(4)]
    y_active = (p > 0) & (yb == a % 2)
    y_to = [(y_active, (down, home + 2 * k, y, c)) for k in range(4)]
    y_from = [(p < 3, (up, 2 * b + k, y, c)) for k in range(2)]
    f_active = last & (zb == y // 4)
    f_to = [(p, z, d % 2 + 2 * (k // 2), k % 2) for k in range(8)]
    f_from = [(p, z, 2 * b + k // 2, k % 2) for k in range(4)]
    ch_to = [(p > 0, (down, *chip_at(2 * c + k // 2), k % 2)) for k in range(4)]
    ch_from = [(p < 3, (up, *chip_at(k), b // 2)) for k in range(4)]
    s1_to = [(p, z0 + k // 4, y0 + (k % 4) // 2, k % 2) for k in range(8)]
    s1_from = [(p, *chip_at(k), home) for k in range(4)]
    quad = 2 * yb + c
    s2_to = [(p, z, 2 * quad + k // 2, k % 2) for k in range(4)]
    s2_from = [(p, z, 2 * k + d // 2, d % 2) for k in range(4)]

    barrier = pltpu.get_barrier_semaphore()
    expected = jnp.int32(4)

    def greet(cond, where):
        @pl.when(cond)
        def _():
            pl.semaphore_signal(barrier, inc=1, device_id=at(*where), device_id_type=MESH)

    pl.semaphore_signal(barrier, inc=1, device_id=at(*core_peer), device_id_type=MESH)
    for where in row_peers:
        pl.semaphore_signal(barrier, inc=1, device_id=at(*where), device_id_type=MESH)
    for cond, where in x_from + y_from + ch_from:
        greet(cond, where)
    for where in f_from:
        greet(last & jnp.logical_not(same(*where)), where)
    for where in s1_from + s2_from:
        greet(jnp.logical_not(same(*where)), where)
    for cond, where in x_to + y_to + ch_to:
        expected = expected + jnp.where(cond, 1, 0)
    for where in f_to:
        expected = expected + jnp.where(f_active & jnp.logical_not(same(*where)), 1, 0)
    for where in s1_to:
        expected = expected + jnp.where((c == home) & jnp.logical_not(same(*where)), 1, 0)
    for where in s2_to:
        expected = expected + jnp.where(jnp.logical_not(same(*where)), 1, 0)

    xst[30:32, :] = jnp.zeros((2, 512), F32)
    xst[0:30, :] = src_ref[0]
    xst[30:31, :] = growth_ref[...]
    fst[...] = jnp.zeros_like(fst)
    fst[0:30, :] = fin_ref[...]
    for g in range(4):
        block = jnp.concatenate([fates_ref[10 * g : 10 * g + 10, :], jnp.zeros((6, 256), F32)], axis=0)
        fates_st[g] = block.astype(BF16)

    pl.semaphore_wait(barrier, expected)

    for k, (cond, where) in enumerate(x_to):
        @pl.when(cond)
        def _(where=where):
            push(xst, xbuf.at[z % 4], in_send, x_sem, at(*where)).start()

    @pl.when(c == home)
    def _():
        pltpu.make_async_copy(xst, xbuf.at[z % 4], x_sem).start()

    for cond, where in y_to:
        @pl.when(cond)
        def _(where=where):
            push(xst, ybuf.at[zb], in_send, y_sem, at(*where)).start()

    slot = t % 4
    fin_dst = ybuf.at[slot // 2, :, pl.ds(pl.multiple_of((slot % 2) * 256, 256), 256)]
    fate_dst = hand.at[:, pl.ds(pl.multiple_of(slot * 256, 256), 256)]
    for where in f_to:
        mine = same(*where)

        @pl.when(f_active & jnp.logical_not(mine))
        def _(where=where):
            push(fst, fin_dst, fs_send, y_sem, at(*where)).start()
            push(fates_st.at[where[2] // 2], fate_dst, fs_send, f_sem, at(*where)).start()

        @pl.when(f_active & mine)
        def _(where=where):
            pltpu.make_async_copy(fst, fin_dst, y_sem).start()
            pltpu.make_async_copy(fates_st.at[where[2] // 2], fate_dst, f_sem).start()

    live_now = jnp.int32(0)
    live_next = jnp.int32(0)
    for k in range(4):
        live_now = live_now + jnp.where(p == k, live_ref[k], 0)
        live_next = live_next + jnp.where(p == k, live_ref[k + 1], 0)
    log_now = jnp.log2(jnp.broadcast_to(live_now.astype(F32), (8, LANES)))
    log_next = jnp.log2(jnp.broadcast_to(live_next.astype(F32), (8, LANES)))
    lanes, subs = lane_iota(), sub_iota()
    row_ids = [HALF * c + LANES * (8 * r + subs) + lanes for r in range(2)]
    col_ids = QUARTER * b + 8 * lanes + subs
    log_b = jnp.where(col_ids < live_next, -log_next, NEG)

    pltpu.make_async_copy(ybuf, ybuf, y_sem).wait()
    keep = lax.broadcasted_iota(jnp.int32, (32, 512), 0) < 30
    for k in range(2):
        cells = jnp.where(keep, ybuf[k], 0.0)
        high, mid, low = three_parts(-2.0 * cells)
        stack = jnp.concatenate([high, mid, low, high], axis=0)
        yt[512 * k : 512 * (k + 1), :] = jnp.transpose(stack)

    for sub in range(8):
        yts[LANES * sub : LANES * (sub + 1), :] = yt[pl.ds(sub, LANES, stride=8), :].astype(BF16)

    def y_norms(k, packed):
        for j in range(16):
            row = pl.multiple_of((16 * k + j) * 8, 8)
            tile = yt[pl.ds(row, 8), :]
            whole = tile + pltpu.roll(tile, 96, axis=1) + pltpu.roll(tile, 64, axis=1)
            whole = jnp.where(lanes < 32, whole, 0.0)
            norm = jnp.broadcast_to(0.25 * jnp.sum(whole * whole, axis=1, keepdims=True), (8, LANES))
            vb[pl.ds(row, 8), :] = norm
            packed = jnp.where(lanes == 16 * k + j, norm, packed)
        return packed

    y_sq = lax.fori_loop(0, 8, y_norms, jnp.zeros((8, LANES), F32))

    pltpu.make_async_copy(xbuf, xbuf, x_sem).wait()
    x_rows = []
    g_rows = []
    for k in range(4):
        cells = jnp.where(keep, xbuf[k], 0.0)
        norms = jnp.sum(cells * cells, axis=0, keepdims=True)
        x_rows += [norms[:, LANES * q : LANES * (q + 1)] for q in range(4)]
        g_rows += [xbuf[k, 30:31, LANES * q : LANES * (q + 1)] for q in range(4)]
        high, mid, low = three_parts(cells)
        none = jnp.zeros_like(high)
        for part, stack in enumerate(([high, high, high, none], [mid, mid, none, low])):
            stack = jnp.concatenate(stack, axis=0)
            xk[LANES * part : LANES * (part + 1), 512 * k : 512 * (k + 1)] = stack.astype(BF16)
            turned = jnp.transpose(stack)
            for q in range(4):
                first = 1024 * (k // 2) + 4 * (k % 2) + q
                (xt0, xt1)[part][pl.ds(first, LANES, stride=8), :] = turned[LANES * q : LANES * (q + 1), :]
    x_sq = [jnp.concatenate(x_rows[8 * r : 8 * r + 8], axis=0) for r in range(2)]
    grown = [jnp.concatenate(g_rows[8 * r : 8 * r + 8], axis=0) for r in range(2)]
    log_a = [jnp.where(row_ids[r] < live_now, jnp.log2(grown[r]) - log_now, NEG) for r in range(2)]
    for r in range(2):
        spread_columns(x_sq[r], ub, 1024 * r)

    def ct_rows(k, carry):
        row = pl.multiple_of(k * 128, 128)
        left = yt[pl.ds(row, 128), :].astype(BF16)
        left = jnp.concatenate([left, left], axis=1)
        cross = jnp.dot(left, xk[...], preferred_element_type=F32)
        for q in range(16):
            norm = vb[pl.ds(row, 128), :] + x_rows[q]
            ct[pl.ds(row, 128), LANES * q : LANES * (q + 1)] = (
                norm + cross[:, LANES * q : LANES * (q + 1)]
            ) * COST_SCALE
        return carry

    lax.fori_loop(0, 8, ct_rows, 0)

    def cr_rows(k, carry):
        row = pl.multiple_of(k * 128, 128)
        left = jnp.concatenate([xt0[pl.ds(row, 128), :], xt1[pl.ds(row, 128), :]], axis=1).astype(BF16)
        right = yts[...]
        right = jnp.concatenate([right, right], axis=1)
        cross = lax.dot_general(left, right, (((1,), (1,)), ((), ())), preferred_element_type=F32)
        for q in range(8):
            norm = ub[pl.ds(row, 128), :] + y_sq[q : q + 1, :]
            cr[pl.ds(row, 128), LANES * q : LANES * (q + 1)] = (
                norm + cross[:, LANES * q : LANES * (q + 1)]
            ) * COST_SCALE
        return carry

    lax.fori_loop(0, 16, cr_rows, 0)

    for r in range(2):
        spread_columns(log_a[r], ub, 1024 * r)

    def iterate(step, carry):
        par = step % 2
        ((m0, s0),) = lse_pass(cr, ub, HALF, 8, 8)
        csend[par, 0:8] = m0
        csend[par, 8:16] = s0
        copy = push(csend.at[par], cslot.at[par], cs_send.at[par], cs_recv.at[par], at(*core_peer))
        copy.start()
        copy.wait()
        m1, s1_ = cslot[par, 0:8], cslot[par, 8:16]
        peak = jnp.maximum(m0, m1)
        total = s0 * jnp.exp2(m0 - peak) + s1_ * jnp.exp2(m1 - peak)
        pot_v = -SHRINK * (peak + jnp.log2(total)) + log_b
        spread_columns(pot_v, vb, 0)
        rows = lse_pass(ct, vb, QUARTER, 16, 4)
        for r in range(2):
            rsend[par, 8 * r : 8 * r + 8] = rows[r][0]
            rsend[par, 16 + 8 * r : 24 + 8 * r] = rows[r][1]
        rslot[par, b] = rsend[par]
        copies = [
            push(rsend.at[par], rslot.at[par, b], rs_send.at[par], rs_recv.at[par], at(*where))
            for where in row_peers
        ]
        for copy in copies:
            copy.start()
        three = rslot.at[par, pl.ds(0, 3)]
        pltpu.make_async_copy(three, three, rs_recv.at[par]).wait()
        out = []
        for r in range(2):
            ms = [rslot[par, k, 8 * r : 8 * r + 8] for k in range(4)]
            ss = [rslot[par, k, 16 + 8 * r : 24 + 8 * r] for k in range(4)]
            peak = jnp.maximum(jnp.maximum(ms[0], ms[1]), jnp.maximum(ms[2], ms[3]))
            total = ss[0] * jnp.exp2(ms[0] - peak)
            for k in range(1, 4):
                total = total + ss[k] * jnp.exp2(ms[k] - peak)
            level = -SHRINK * (peak + jnp.log2(total))
            spread_columns(level + log_a[r], ub, 1024 * r)
            out += [peak, total, level]
        pltpu.make_async_copy(three, three, rs_send.at[par]).wait()
        return tuple(out)

    zero = jnp.zeros((8, LANES), F32)
    final = lax.fori_loop(0, ITERS, iterate, (zero,) * 6)

    for r in range(2):
        fsend[8 * r : 8 * r + 8] = final[3 * r + 2] * (EPS / LOG2E)
    pot_copy = push(fsend, fother, p_send, p_recv, at(*core_peer))
    pot_copy.start()

    wpeak = []
    wscale = []
    for r in range(2):
        inv = 1.0 / final[3 * r + 1]
        for q in range(8):
            wpeak.append(final[3 * r][q : q + 1, :])
            wscale.append(inv[q : q + 1, :])

    def w_rows(k, carry):
        row = pl.multiple_of(k * 16, 16)
        left = vb[pl.ds(row, 16), :]
        for q in range(16):
            s = left - ct[pl.ds(row, 16), LANES * q : LANES * (q + 1)]
            w = jnp.exp2(s - wpeak[q]) * wscale[q]
            wt[pl.ds(row, 16), LANES * q : LANES * (q + 1)] = w.astype(BF16)
        return carry

    lax.fori_loop(0, QUARTER // 16, w_rows, 0)

    @pl.when(last)
    def _():
        pltpu.make_async_copy(hand, hand, f_sem).wait()

    @pl.when(jnp.logical_not(last))
    def _():
        pltpu.make_async_copy(chin, chin, ch_recv).wait()
        total = chin[0].astype(F32)
        for k in range(1, 4):
            total = total + chin[k].astype(F32)
        hand[...] = total.astype(BF16)

    ids = HALF * c + lax.broadcasted_iota(jnp.int32, (16, HALF), 1)
    part = jnp.dot(hand[...], wt[...], preferred_element_type=F32)
    part = jnp.where(ids < live_now, part, 0.0)
    pbuf[...] = part
    pbf[0] = part[:, 0:QUARTER].astype(BF16)
    pbf[1] = part[:, QUARTER:HALF].astype(BF16)
    for k, (cond, where) in enumerate(ch_to):
        @pl.when(cond)
        def _(k=k, where=where):
            push(pbf.at[k // 2], chin.at[b], ch_send, ch_recv, at(*where)).start()

    def s1_src(k):
        first = pl.multiple_of(QUARTER * (a % 2) + LANES * k, LANES)
        return pbuf.at[:, pl.ds(first, LANES)]

    for k, where in enumerate(s1_to):
        mine = same(*where)

        @pl.when((c == home) & jnp.logical_not(mine))
        def _(k=k, where=where):
            push(s1_src(k), s1.at[b], s1_send, s1_recv, at(*where)).start()

        @pl.when((c == home) & mine)
        def _(k=k):
            pltpu.make_async_copy(s1_src(k), s1.at[b], s1_recv).start()

    pltpu.make_async_copy(s1, s1, s1_recv).wait()
    s2st[...] = (s1[0] + s1[1]) + (s1[2] + s1[3])
    for where in s2_to:
        mine = same(*where)

        @pl.when(jnp.logical_not(mine))
        def _(where=where):
            push(s2st, s2.at[d], s2_send, s2_recv, at(*where)).start()

        @pl.when(mine)
        def _():
            pltpu.make_async_copy(s2st, s2.at[d], s2_recv).start()

    pot_copy.wait()
    own = jnp.where(c == home, fsend[...], fother[...])
    picked = own[0:4]
    for k in range(1, 4):
        picked = jnp.where(z % 4 == k, own[4 * k : 4 * k + 4], picked)
    for k in range(4):
        pot_ref[0:1, LANES * k : LANES * (k + 1)] = picked[k : k + 1]

    pltpu.make_async_copy(s2, s2, s2_recv).wait()
    turn = lax.rem(LANES - 32 * quad, LANES)
    for g in range(4):
        out_ref[0, 10 * g : 10 * g + 10, :] = pltpu.roll(s2[g], turn, axis=1)[0:10, 0:32]

    def settle(cond, ref, sem):
        @pl.when(cond)
        def _():
            pltpu.make_async_copy(ref, ref, sem).wait()

    for cond, where in x_to + y_to:
        settle(cond, xst, in_send)
    for where in f_to:
        off = f_active & jnp.logical_not(same(*where))
        settle(off, fst, fs_send)
        settle(off, fates_st.at[0], fs_send)
    for cond, where in ch_to:
        settle(cond, pbf.at[0], ch_send)
    for where in s1_to:
        settle((c == home) & jnp.logical_not(same(*where)), s2st, s1_send)
    for where in s2_to:
        settle(jnp.logical_not(same(*where)), s2st, s2_send)


def local(src_cells, final_cells, growth, live, final_fates):
    vmem = pl.BlockSpec(memory_space=pltpu.VMEM)
    dma = pltpu.SemaphoreType.DMA
    V = pltpu.VMEM
    return tuple(pl.pallas_call(
        kernel,
        out_shape=(
            jax.ShapeDtypeStruct((1, 40, 32), F32),
            jax.ShapeDtypeStruct((1, 512), F32),
        ),
        in_specs=[vmem, vmem, vmem, pl.BlockSpec(memory_space=pltpu.SMEM), vmem],
        out_specs=(vmem, vmem),
        scratch_shapes=[
            V((32, 512), F32), V((32, 256), F32), V((4, 16, 256), BF16),
            V((4, 32, 512), F32), V((2, 32, 512), F32),
            V((256, HALF), BF16), V((HALF, 128), F32), V((HALF, 128), F32), V((QUARTER, 128), F32), V((QUARTER, 128), BF16),
            V((QUARTER, HALF), F32), V((HALF, QUARTER), F32),
            V((HALF, 128), F32), V((QUARTER, 128), F32), V((QUARTER, HALF), BF16),
            V((2, 16, 128), F32), V((2, 16, 128), F32), V((2, 32, 128), F32), V((2, 4, 32, 128), F32),
            V((16, 128), F32), V((16, 128), F32),
            V((16, QUARTER), BF16), V((16, HALF), F32), V((2, 16, QUARTER), BF16), V((4, 16, QUARTER), BF16),
            V((4, 16, 128), F32), V((16, 128), F32), V((4, 16, 128), F32),
            dma(()), dma(()), dma(()), dma(()), dma(()), dma((2,)), dma((2,)), dma((2,)), dma((2,)),
            dma(()), dma(()), dma(()), dma(()), dma(()), dma(()), dma(()), dma(()),
        ],
        compiler_params=pltpu.CompilerParams(
            collective_id=0, has_side_effects=True, vmem_limit_bytes=48 * 2**20
        ),
        name="transport",
    )(src_cells, final_cells, growth, live, final_fates))


def solution(mesh):
    placed = (P("pair", None, "src"), P(None, "tgt"), P("pair", "src"), P(), P(None, "tgt"))
    return jax.shard_map(
        local,
        mesh=mesh,
        in_specs=placed,
        out_specs=(P("pair", None, ("src", "tgt")), P("pair", "src")),
        check_vma=False,
    )
```

```python
import functools
import math

import jax
import jax.numpy as jnp
from jax import lax
from jax.experimental import pallas as pl
from jax.experimental.pallas import tpu as pltpu
from jax.sharding import PartitionSpec as P

MESH = pl.DeviceIdType.MESH
F32 = jnp.float32
BF16 = jnp.bfloat16

ITERS = 8
EPS = 0.1
LAM = 1.0
NEG = -1e30
SHRINK = LAM / (LAM + EPS)
LOG2E = 1.0 / math.log(2.0)
COST_SCALE = LOG2E / (EPS * 60.0)
LOWEST = -3e38

HALF = 2048
QUARTER = 1024
LANES = 128
GROUP = 32


def lane_iota():
    return lax.broadcasted_iota(jnp.int32, (8, LANES), 1)


def sub_iota():
    return lax.broadcasted_iota(jnp.int32, (8, LANES), 0)


def spread_columns(packed, dst, base):
    for t in range(LANES):
        row = pl.multiple_of(base + 8 * t, 8)
        dst[pl.ds(row, 8), :] = jnp.broadcast_to(packed[:, t : t + 1], (8, LANES))


def lse_pass(cost, spread, row0, lane0):
    tiles = 8

    def walk(start, update):
        def body(k, acc):
            acc = list(acc)
            for t in range(GROUP):
                row = pl.multiple_of(row0 + (k * GROUP + t) * 8, 8)
                left = spread[pl.ds(row, 8), :]
                for q in range(tiles):
                    lane = pl.multiple_of(lane0 + LANES * q, LANES)
                    acc[q] = update(q, acc[q], left - cost[pl.ds(row, 8), pl.ds(lane, LANES)])
            return tuple(acc)

        return lax.fori_loop(0, QUARTER // (8 * GROUP), body, tuple(start))

    peaks = walk([jnp.full((8, LANES), LOWEST, F32)] * tiles, lambda q, a, s: jnp.maximum(a, s))
    peaks = [jnp.broadcast_to(jnp.max(a, axis=0, keepdims=True), (8, LANES)) for a in peaks]
    sums = walk([jnp.zeros((8, LANES), F32)] * tiles, lambda q, a, s: a + jnp.exp2(s - peaks[q]))
    sums = [jnp.broadcast_to(jnp.sum(a, axis=0, keepdims=True), (8, LANES)) for a in sums]
    which = sub_iota()
    m, s = peaks[0], sums[0]
    for q in range(1, 8):
        m = jnp.where(which == q, peaks[q], m)
        s = jnp.where(which == q, sums[q], s)
    return m, s


def three_parts(x):
    high = x.astype(BF16).astype(F32)
    rest = x - high
    mid = rest.astype(BF16).astype(F32)
    low = (rest - mid).astype(BF16).astype(F32)
    return high, mid, low


def kernel(
    src_ref, fin_ref, growth_ref, live_ref, fates_ref, out_ref, pot_ref,
    xst, fst, fates_st, xbuf, ybuf, xk, xt0, xt1, yt, yk, ysq, la, ct, cr, ub, vb, wt,
    csend, cslot, rsend, rslot, fsend, fother, hand, pbuf, pbf, chin, s1, s2st, s2,
    in_send, x_sem, y_sem, f_sem, fs_send, cs_send, cs_recv, rs_send, rs_recv,
    p_send, p_recv, ch_send, ch_recv, s1_send, s1_recv, s2_send, s2_recv,
):
    p = lax.axis_index("pair")
    z = lax.axis_index("src")
    t = lax.axis_index("tgt")
    y, c = t // 2, t % 2
    zb, yb = z % 2, y % 2
    b = 2 * zb + yb
    z0, y0 = z - zb, y - yb
    a, d = z // 2, y // 2
    home = z // 4
    last = p == 3

    def at(pp, zz, yy, cc):
        return {"pair": pp, "src": zz, "tgt": 2 * yy + cc}

    def push(src, dst, send, recv, where):
        return pltpu.make_async_remote_copy(src, dst, send, recv, device_id=where, device_id_type=MESH)

    def same(pp, zz, yy, cc):
        return (pp == p) & (zz == z) & (yy == y) & (cc == c)

    up, down = jnp.minimum(p + 1, 3), jnp.maximum(p - 1, 0)
    chips = [((b + k) % 4) for k in range(1, 4)]
    chip_at = lambda bb: (z0 + bb // 2, y0 + bb % 2)
    core_peer = (p, z, y, 1 - c)
    row_peers = [(p, *chip_at(bb), c) for bb in chips]
    x_to = [(c == home, (p, (z + k) % 8, y, c)) for k in range(1, 8)]
    x_from = [(4 * c + k != z, (p, 4 * c + k, y, c)) for k in range(4)]
    y_active = (p > 0) & (yb == a % 2)
    y_to = [(y_active, (down, home + 2 * k, y, c)) for k in range(4)]
    y_from = [(p < 3, (up, 2 * b + k, y, c)) for k in range(2)]
    f_active = last & (zb == y // 4)
    f_to = [(p, z, d % 2 + 2 * (k // 2), k % 2) for k in range(8)]
    f_from = [(p, z, 2 * b + k // 2, k % 2) for k in range(4)]
    ch_to = [(p > 0, (down, *chip_at(2 * c + k // 2), k % 2)) for k in range(4)]
    ch_from = [(p < 3, (up, *chip_at(k), b // 2)) for k in range(4)]
    s1_to = [(p, z0 + k // 4, y0 + (k % 4) // 2, k % 2) for k in range(8)]
    s1_from = [(p, *chip_at(k), home) for k in range(4)]
    quad = 2 * yb + c
    s2_to = [(p, z, 2 * quad + k // 2, k % 2) for k in range(4)]
    s2_from = [(p, z, 2 * k + d // 2, d % 2) for k in range(4)]

    barrier = pltpu.get_barrier_semaphore()
    expected = jnp.int32(4)

    def greet(cond, where):
        @pl.when(cond)
        def _():
            pl.semaphore_signal(barrier, inc=1, device_id=at(*where), device_id_type=MESH)

    pl.semaphore_signal(barrier, inc=1, device_id=at(*core_peer), device_id_type=MESH)
    for where in row_peers:
        pl.semaphore_signal(barrier, inc=1, device_id=at(*where), device_id_type=MESH)
    for cond, where in x_from + y_from + ch_from:
        greet(cond, where)
    for where in f_from:
        greet(last & jnp.logical_not(same(*where)), where)
    for where in s1_from + s2_from:
        greet(jnp.logical_not(same(*where)), where)
    for cond, where in x_to + y_to + ch_to:
        expected = expected + jnp.where(cond, 1, 0)
    for where in f_to:
        expected = expected + jnp.where(f_active & jnp.logical_not(same(*where)), 1, 0)
    for where in s1_to:
        expected = expected + jnp.where((c == home) & jnp.logical_not(same(*where)), 1, 0)
    for where in s2_to:
        expected = expected + jnp.where(jnp.logical_not(same(*where)), 1, 0)

    xst[30:32, :] = jnp.zeros((2, 512), F32)
    xst[0:30, :] = src_ref[0]
    xst[30:31, :] = growth_ref[...]
    fst[...] = jnp.zeros_like(fst)
    fst[0:30, :] = fin_ref[...]
    for g in range(4):
        block = jnp.concatenate([fates_ref[10 * g : 10 * g + 10, :], jnp.zeros((6, 256), F32)], axis=0)
        fates_st[g] = block.astype(BF16)

    pl.semaphore_wait(barrier, expected)

    for cond, where in y_to:
        @pl.when(cond)
        def _(where=where):
            push(xst, ybuf.at[zb], in_send, y_sem, at(*where)).start()

    slot = t % 4
    fin_dst = ybuf.at[slot // 2, :, pl.ds(pl.multiple_of((slot % 2) * 256, 256), 256)]
    fate_dst = hand.at[:, pl.ds(pl.multiple_of(slot * 256, 256), 256)]
    for where in f_to:
        mine = same(*where)

        @pl.when(f_active & jnp.logical_not(mine))
        def _(where=where):
            push(fst, fin_dst, fs_send, y_sem, at(*where)).start()
            push(fates_st.at[where[2] // 2], fate_dst, fs_send, f_sem, at(*where)).start()

        @pl.when(f_active & mine)
        def _(where=where):
            pltpu.make_async_copy(fst, fin_dst, y_sem).start()
            pltpu.make_async_copy(fates_st.at[where[2] // 2], fate_dst, f_sem).start()

    for k, (cond, where) in enumerate(x_to):
        @pl.when(cond)
        def _(where=where):
            push(xst, xbuf.at[z % 4], in_send, x_sem.at[z % 4], at(*where)).start()

    @pl.when(c == home)
    def _():
        pltpu.make_async_copy(xst, xbuf.at[z % 4], x_sem.at[z % 4]).start()

    live_now = jnp.int32(0)
    live_next = jnp.int32(0)
    for k in range(4):
        live_now = live_now + jnp.where(p == k, live_ref[k], 0)
        live_next = live_next + jnp.where(p == k, live_ref[k + 1], 0)
    log_now = jnp.log2(jnp.broadcast_to(live_now.astype(F32), (8, LANES)))
    log_next = jnp.log2(jnp.broadcast_to(live_next.astype(F32), (8, LANES)))
    lanes, subs = lane_iota(), sub_iota()
    row_ids = [HALF * c + LANES * (8 * r + subs) + lanes for r in range(2)]
    col_ids = QUARTER * b + 8 * lanes + subs
    log_b = jnp.where(col_ids < live_next, -log_next, NEG)

    pltpu.make_async_copy(ybuf, ybuf, y_sem).wait()
    row_of = lax.broadcasted_iota(jnp.int32, (32, 512), 0)
    keep = row_of < 30
    for k in range(2):
        cells = jnp.where(keep, ybuf[k], 0.0)
        norms = jnp.sum(cells * cells, axis=0, keepdims=True)
        for q in range(4):
            flat = jnp.broadcast_to(norms[:, LANES * q : LANES * (q + 1)], (LANES, LANES))
            first = 512 * k + LANES * q
            vb[first : first + LANES, :] = jnp.transpose(flat)
        high, mid, low = three_parts(-2.0 * cells)
        stack = jnp.concatenate([jnp.where(row_of == 30, norms, high), mid, low, high], axis=0)
        yt[512 * k : 512 * (k + 1), :] = jnp.transpose(stack)
    for sub in range(8):
        turned = jnp.transpose(yt[pl.ds(sub, LANES, stride=8), :])
        yk[:, LANES * sub : LANES * (sub + 1)] = turned.astype(BF16)
        ysq[sub : sub + 1, :] = turned[30:31, :]

    def merge(first, second):
        peak = jnp.maximum(first[0], second[0])
        return peak, first[1] * jnp.exp2(first[0] - peak) + second[1] * jnp.exp2(second[0] - peak)

    columns = None
    for r in range(2):
        x_rows = []
        g_rows = []
        for k in range(2 * r, 2 * r + 2):
            block = xbuf.at[k]
            pltpu.make_async_copy(block, block, x_sem.at[k]).wait()
            cells = jnp.where(keep, xbuf[k], 0.0)
            norms = jnp.sum(cells * cells, axis=0, keepdims=True)
            x_rows += [norms[:, LANES * q : LANES * (q + 1)] for q in range(4)]
            g_rows += [xbuf[k, 30:31, LANES * q : LANES * (q + 1)] for q in range(4)]
            high, mid, low = three_parts(cells)
            none = jnp.zeros_like(high)
            for part, stack in enumerate(([high, high, high, none], [mid, mid, none, low])):
                stack = jnp.concatenate(stack, axis=0)
                xk[LANES * part : LANES * (part + 1), 512 * k : 512 * (k + 1)] = stack.astype(BF16)
                turned = jnp.transpose(stack)
                for q in range(4):
                    first = 1024 * r + 4 * (k % 2) + q
                    (xt0, xt1)[part][pl.ds(first, LANES, stride=8), :] = turned[LANES * q : LANES * (q + 1), :]
        grown = jnp.concatenate(g_rows, axis=0)
        log_a = jnp.where(row_ids[r] < live_now, jnp.log2(grown) - log_now, NEG)
        la[r] = log_a
        spread_columns(jnp.concatenate(x_rows, axis=0), ub, 1024 * r)

        def ct_rows(k, carry, r=r, x_rows=x_rows):
            row = pl.multiple_of(k * 256, 256)
            left = yt[pl.ds(row, 256), :].astype(BF16)
            left = jnp.concatenate([left, left], axis=1)
            cross = jnp.dot(left, xk[:, 1024 * r : 1024 * (r + 1)], preferred_element_type=F32)
            for q in range(8):
                norm = vb[pl.ds(row, 256), :] + x_rows[q]
                first = 1024 * r + LANES * q
                ct[pl.ds(row, 256), first : first + LANES] = (
                    norm + cross[:, LANES * q : LANES * (q + 1)]
                ) * COST_SCALE
            return carry

        lax.fori_loop(0, 4, ct_rows, 0)

        def cr_rows(k, carry, r=r):
            row = pl.multiple_of(1024 * r + k * 256, 256)
            left = jnp.concatenate([xt0[pl.ds(row, 256), :], xt1[pl.ds(row, 256), :]], axis=1).astype(BF16)
            right = yk[...]
            cross = jnp.dot(left, jnp.concatenate([right, right], axis=0), preferred_element_type=F32)
            for q in range(8):
                norm = ub[pl.ds(row, 256), :] + ysq[q : q + 1, :]
                cr[pl.ds(row, 256), LANES * q : LANES * (q + 1)] = (
                    norm + cross[:, LANES * q : LANES * (q + 1)]
                ) * COST_SCALE
            return carry

        lax.fori_loop(0, 4, cr_rows, 0)
        spread_columns(log_a, ub, 1024 * r)
        found = lse_pass(cr, ub, 1024 * r, 0)
        columns = found if columns is None else merge(columns, found)

    def from_columns(par, m0, s0):
        csend[par, 0:8] = m0
        csend[par, 8:16] = s0
        copy = push(csend.at[par], cslot.at[par], cs_send.at[par], cs_recv.at[par], at(*core_peer))
        copy.start()
        copy.wait()
        peak, total = merge((m0, s0), (cslot[par, 0:8], cslot[par, 8:16]))
        spread_columns(-SHRINK * (peak + jnp.log2(total)) + log_b, vb, 0)

    def send_rows(par):
        def half(r, carry):
            m, s = lse_pass(ct, vb, 0, 1024 * r)
            rsend[par, r, 0:8] = m
            rsend[par, r, 8:16] = s
            rslot[par, r, b, 0:8] = m
            rslot[par, r, b, 8:16] = s
            for where in row_peers:
                push(
                    rsend.at[par, r], rslot.at[par, r, b], rs_send.at[par, r], rs_recv.at[par, r], at(*where)
                ).start()
            return carry

        lax.fori_loop(0, 2, half, 0)

    def from_rows(par, r):
        three = rslot.at[par, r, pl.ds(0, 3)]
        pltpu.make_async_copy(three, three, rs_recv.at[par, r]).wait()
        pltpu.make_async_copy(three, three, rs_send.at[par, r]).wait()
        ms = [rslot[par, r, k, 0:8] for k in range(4)]
        ss = [rslot[par, r, k, 8:16] for k in range(4)]
        peak = jnp.maximum(jnp.maximum(ms[0], ms[1]), jnp.maximum(ms[2], ms[3]))
        terms = [ss[k] * jnp.exp2(ms[k] - peak) for k in range(4)]
        total = (terms[0] + terms[1]) + (terms[2] + terms[3])
        return peak, total, -SHRINK * (peak + jnp.log2(total))

    def iterate(step, carry):
        par = step % 2
        from_columns(par, *carry)
        send_rows(par)

        def half(r, so_far):
            level = from_rows(par, r)[2]
            spread_columns(level + la[r], ub, 1024 * r)
            return merge(so_far, lse_pass(cr, ub, 1024 * r, 0))

        return lax.fori_loop(0, 2, half, (jnp.full((8, LANES), LOWEST, F32), jnp.zeros((8, LANES), F32)))

    columns = lax.fori_loop(0, ITERS - 1, iterate, columns)
    par = (ITERS - 1) % 2
    from_columns(par, *columns)
    send_rows(par)

    for r in range(2):
        wpeak = [rsend[par, r, q : q + 1, :] for q in range(8)]

        def w_rows(k, carry, r=r, wpeak=wpeak):
            for j in range(4):
                row = pl.multiple_of(k * 64 + 16 * j, 16)
                left = vb[pl.ds(row, 16), :]
                for q in range(8):
                    first = 1024 * r + LANES * q
                    s = left - ct[pl.ds(row, 16), first : first + LANES]
                    wt[pl.ds(row, 16), first : first + LANES] = jnp.exp2(s - wpeak[q]).astype(BF16)
            return carry

        lax.fori_loop(0, QUARTER // 64, w_rows, 0)

    scales = []
    for r in range(2):
        peak, total, level = from_rows(par, r)
        fsend[8 * r : 8 * r + 8] = level * (EPS / LOG2E)
        scale = jnp.exp2(rsend[par, r, 0:8] - peak) / total
        scale = jnp.where(row_ids[r] < live_now, scale, 0.0)
        scales += [scale[q : q + 1, :] for q in range(8)]

    pot_copy = push(fsend, fother, p_send, p_recv, at(*core_peer))
    pot_copy.start()

    @pl.when(last)
    def _():
        pltpu.make_async_copy(hand, hand, f_sem).wait()

    @pl.when(jnp.logical_not(last))
    def _():
        pltpu.make_async_copy(chin, chin, ch_recv).wait()
        total = chin[0].astype(F32)
        for k in range(1, 4):
            total = total + chin[k].astype(F32)
        hand[...] = total.astype(BF16)

    for r in range(2):
        part = jnp.dot(hand[...], wt[:, 1024 * r : 1024 * (r + 1)], preferred_element_type=F32)
        for q in range(8):
            tile = part[:, LANES * q : LANES * (q + 1)] * scales[8 * r + q]
            pbuf[:, 1024 * r + LANES * q : 1024 * r + LANES * (q + 1)] = tile
            pbf[r, :, LANES * q : LANES * (q + 1)] = tile.astype(BF16)
    for k, (cond, where) in enumerate(ch_to):
        @pl.when(cond)
        def _(k=k, where=where):
            push(pbf.at[k // 2], chin.at[b], ch_send, ch_recv, at(*where)).start()

    def s1_src(k):
        first = pl.multiple_of(QUARTER * (a % 2) + LANES * k, LANES)
        return pbuf.at[:, pl.ds(first, LANES)]

    for k, where in enumerate(s1_to):
        mine = same(*where)

        @pl.when((c == home) & jnp.logical_not(mine))
        def _(k=k, where=where):
            push(s1_src(k), s1.at[b], s1_send, s1_recv, at(*where)).start()

        @pl.when((c == home) & mine)
        def _(k=k):
            pltpu.make_async_copy(s1_src(k), s1.at[b], s1_recv).start()

    pltpu.make_async_copy(s1, s1, s1_recv).wait()
    s2st[...] = (s1[0] + s1[1]) + (s1[2] + s1[3])
    for where in s2_to:
        mine = same(*where)

        @pl.when(jnp.logical_not(mine))
        def _(where=where):
            push(s2st, s2.at[d], s2_send, s2_recv, at(*where)).start()

        @pl.when(mine)
        def _():
            pltpu.make_async_copy(s2st, s2.at[d], s2_recv).start()

    pot_copy.wait()
    own = jnp.where(c == home, fsend[...], fother[...])
    picked = own[0:4]
    for k in range(1, 4):
        picked = jnp.where(z % 4 == k, own[4 * k : 4 * k + 4], picked)
    for k in range(4):
        pot_ref[0:1, LANES * k : LANES * (k + 1)] = picked[k : k + 1]

    pltpu.make_async_copy(s2, s2, s2_recv).wait()
    turn = lax.rem(LANES - 32 * quad, LANES)
    for g in range(4):
        out_ref[0, 10 * g : 10 * g + 10, :] = pltpu.roll(s2[g], turn, axis=1)[0:10, 0:32]

    def settle(cond, ref, sem):
        @pl.when(cond)
        def _():
            pltpu.make_async_copy(ref, ref, sem).wait()

    for cond, where in x_to + y_to:
        settle(cond, xst, in_send)
    for where in f_to:
        off = f_active & jnp.logical_not(same(*where))
        settle(off, fst, fs_send)
        settle(off, fates_st.at[0], fs_send)
    for cond, where in ch_to:
        settle(cond, pbf.at[0], ch_send)
    for where in s1_to:
        settle((c == home) & jnp.logical_not(same(*where)), s2st, s1_send)
    for where in s2_to:
        settle(jnp.logical_not(same(*where)), s2st, s2_send)


def local(src_cells, final_cells, growth, live, final_fates):
    vmem = pl.BlockSpec(memory_space=pltpu.VMEM)
    dma = pltpu.SemaphoreType.DMA
    V = pltpu.VMEM
    return tuple(pl.pallas_call(
        kernel,
        out_shape=(
            jax.ShapeDtypeStruct((1, 40, 32), F32),
            jax.ShapeDtypeStruct((1, 512), F32),
        ),
        in_specs=[vmem, vmem, vmem, pl.BlockSpec(memory_space=pltpu.SMEM), vmem],
        out_specs=(vmem, vmem),
        scratch_shapes=[
            V((32, 512), F32), V((32, 256), F32), V((4, 16, 256), BF16),
            V((4, 32, 512), F32), V((2, 32, 512), F32),
            V((256, HALF), BF16), V((HALF, 128), F32), V((HALF, 128), F32), V((QUARTER, 128), F32), V((128, QUARTER), BF16),
            V((8, 128), F32), V((2, 8, 128), F32),
            V((QUARTER, HALF), F32), V((HALF, QUARTER), F32),
            V((HALF, 128), F32), V((QUARTER, 128), F32), V((QUARTER, HALF), BF16),
            V((2, 16, 128), F32), V((2, 16, 128), F32), V((2, 2, 16, 128), F32), V((2, 2, 4, 16, 128), F32),
            V((16, 128), F32), V((16, 128), F32),
            V((16, QUARTER), BF16), V((16, HALF), F32), V((2, 16, QUARTER), BF16), V((4, 16, QUARTER), BF16),
            V((4, 16, 128), F32), V((16, 128), F32), V((4, 16, 128), F32),
            dma(()), dma((4,)), dma(()), dma(()), dma(()), dma((2,)), dma((2,)), dma((2, 2)), dma((2, 2)),
            dma(()), dma(()), dma(()), dma(()), dma(()), dma(()), dma(()), dma(()),
        ],
        compiler_params=pltpu.CompilerParams(
            collective_id=0, has_side_effects=True, vmem_limit_bytes=48 * 2**20
        ),
        name="transport",
    )(src_cells, final_cells, growth, live, final_fates))


def solution(mesh):
    placed = (P("pair", None, "src"), P(None, "tgt"), P("pair", "src"), P(), P(None, "tgt"))
    return jax.shard_map(
        local,
        mesh=mesh,
        in_specs=placed,
        out_specs=(P("pair", None, ("src", "tgt")), P("pair", "src")),
        check_vma=False,
    )
```

```python
import functools
import math

import jax
import jax.numpy as jnp
from jax import lax
from jax.experimental import pallas as pl
from jax.experimental.pallas import tpu as pltpu
from jax.sharding import PartitionSpec as P

MESH = pl.DeviceIdType.MESH
F32 = jnp.float32
BF16 = jnp.bfloat16

ITERS = 8
EPS = 0.1
LAM = 1.0
NEG = -1e30
SHRINK = LAM / (LAM + EPS)
LOG2E = 1.0 / math.log(2.0)
COST_SCALE = LOG2E / (EPS * 60.0)
LOWEST = -3e38

HALF = 2048
QUARTER = 1024
LANES = 128
GROUP = 32


def lane_iota():
    return lax.broadcasted_iota(jnp.int32, (8, LANES), 1)


def sub_iota():
    return lax.broadcasted_iota(jnp.int32, (8, LANES), 0)


def spread_columns(packed, dst):
    for t in range(LANES):
        dst[8 * t : 8 * t + 8, :] = jnp.broadcast_to(packed[:, t : t + 1], (8, LANES))


def lse_pass(cost, spread):
    tiles = 8
    rows = 8 * GROUP

    def walk(start, update):
        def body(k, acc):
            acc = list(acc)
            first = pl.multiple_of(k * rows, rows)
            left_rows = spread.at[pl.ds(first, rows)]
            cost_rows = cost.at[pl.ds(first, rows)]
            for t in range(GROUP):
                left = left_rows[8 * t : 8 * t + 8, :]
                for q in range(tiles):
                    acc[q] = update(q, acc[q], left - cost_rows[8 * t : 8 * t + 8, LANES * q : LANES * (q + 1)])
            return tuple(acc)

        return lax.fori_loop(0, QUARTER // rows, body, tuple(start))

    peaks = walk([jnp.full((8, LANES), LOWEST, F32)] * tiles, lambda q, a, s: jnp.maximum(a, s))
    peaks = [jnp.broadcast_to(jnp.max(a, axis=0, keepdims=True), (8, LANES)) for a in peaks]
    sums = walk([jnp.zeros((8, LANES), F32)] * tiles, lambda q, a, s: a + jnp.exp2(s - peaks[q]))
    sums = [jnp.broadcast_to(jnp.sum(a, axis=0, keepdims=True), (8, LANES)) for a in sums]
    which = sub_iota()
    m, s = peaks[0], sums[0]
    for q in range(1, 8):
        m = jnp.where(which == q, peaks[q], m)
        s = jnp.where(which == q, sums[q], s)
    return m, s


def three_parts(x):
    high = x.astype(BF16).astype(F32)
    rest = x - high
    mid = rest.astype(BF16).astype(F32)
    low = (rest - mid).astype(BF16).astype(F32)
    return high, mid, low


def kernel(
    src_ref, fin_ref, growth_ref, live_ref, fates_ref, out_ref, pot_ref,
    xst, fst, fates_st, xbuf, ybuf, xk, xt0, xt1, yt, yk, ysq, la, ct, cr, ub, vb, wt,
    csend, cslot, rsend, rslot, fsend, fother, hand, pbuf, pbf, chin, s1, s2st, s2,
    in_send, x_sem, y_sem, f_sem, fs_send, cs_send, cs_recv, rs_send, rs_recv,
    p_send, p_recv, ch_send, ch_recv, s1_send, s1_recv, s2_send, s2_recv,
):
    p = lax.axis_index("pair")
    z = lax.axis_index("src")
    t = lax.axis_index("tgt")
    y, c = t // 2, t % 2
    zb, yb = z % 2, y % 2
    b = 2 * zb + yb
    z0, y0 = z - zb, y - yb
    a, d = z // 2, y // 2
    home = z // 4
    last = p == 3

    def at(pp, zz, yy, cc):
        return {"pair": pp, "src": zz, "tgt": 2 * yy + cc}

    def push(src, dst, send, recv, where):
        return pltpu.make_async_remote_copy(src, dst, send, recv, device_id=where, device_id_type=MESH)

    def same(pp, zz, yy, cc):
        return (pp == p) & (zz == z) & (yy == y) & (cc == c)

    up, down = jnp.minimum(p + 1, 3), jnp.maximum(p - 1, 0)
    chips = [((b + k) % 4) for k in range(1, 4)]
    chip_at = lambda bb: (z0 + bb // 2, y0 + bb % 2)
    core_peer = (p, z, y, 1 - c)
    row_peers = [(p, *chip_at(bb), c) for bb in chips]
    x_to = [(c == home, (p, (z + k) % 8, y, c)) for k in range(1, 8)]
    x_from = [(4 * c + k != z, (p, 4 * c + k, y, c)) for k in range(4)]
    y_active = (p > 0) & (yb == a % 2)
    y_to = [(y_active, (down, home + 2 * k, y, c)) for k in range(4)]
    y_from = [(p < 3, (up, 2 * b + k, y, c)) for k in range(2)]
    f_active = last & (zb == y // 4)
    f_to = [(p, z, d % 2 + 2 * (k // 2), k % 2) for k in range(8)]
    f_from = [(p, z, 2 * b + k // 2, k % 2) for k in range(4)]
    ch_to = [(p > 0, (down, *chip_at(2 * c + k // 2), k % 2)) for k in range(4)]
    ch_from = [(p < 3, (up, *chip_at(k), b // 2)) for k in range(4)]
    s1_to = [(p, z0 + k // 4, y0 + (k % 4) // 2, k % 2) for k in range(8)]
    s1_from = [(p, *chip_at(k), home) for k in range(4)]
    quad = 2 * yb + c
    s2_to = [(p, z, 2 * quad + k // 2, k % 2) for k in range(4)]
    s2_from = [(p, z, 2 * k + d // 2, d % 2) for k in range(4)]

    barrier = pltpu.get_barrier_semaphore()
    expected = jnp.int32(4)

    def greet(cond, where):
        @pl.when(cond)
        def _():
            pl.semaphore_signal(barrier, inc=1, device_id=at(*where), device_id_type=MESH)

    pl.semaphore_signal(barrier, inc=1, device_id=at(*core_peer), device_id_type=MESH)
    for where in row_peers:
        pl.semaphore_signal(barrier, inc=1, device_id=at(*where), device_id_type=MESH)
    for cond, where in x_from + y_from + ch_from:
        greet(cond, where)
    for where in f_from:
        greet(last & jnp.logical_not(same(*where)), where)
    for where in s1_from + s2_from:
        greet(jnp.logical_not(same(*where)), where)
    for cond, where in x_to + y_to + ch_to:
        expected = expected + jnp.where(cond, 1, 0)
    for where in f_to:
        expected = expected + jnp.where(f_active & jnp.logical_not(same(*where)), 1, 0)
    for where in s1_to:
        expected = expected + jnp.where((c == home) & jnp.logical_not(same(*where)), 1, 0)
    for where in s2_to:
        expected = expected + jnp.where(jnp.logical_not(same(*where)), 1, 0)

    xst[30:32, :] = jnp.zeros((2, 512), F32)
    xst[0:30, :] = src_ref[0]
    xst[30:31, :] = growth_ref[...]
    fst[...] = jnp.zeros_like(fst)
    fst[0:30, :] = fin_ref[...]
    for g in range(4):
        block = jnp.concatenate([fates_ref[10 * g : 10 * g + 10, :], jnp.zeros((6, 256), F32)], axis=0)
        fates_st[g] = block.astype(BF16)

    pl.semaphore_wait(barrier, expected)

    for cond, where in y_to:
        @pl.when(cond)
        def _(where=where):
            push(xst, ybuf.at[zb], in_send, y_sem, at(*where)).start()

    slot = t % 4
    fin_dst = ybuf.at[slot // 2, :, pl.ds(pl.multiple_of((slot % 2) * 256, 256), 256)]
    fate_dst = hand.at[:, pl.ds(pl.multiple_of(slot * 256, 256), 256)]
    for where in f_to:
        mine = same(*where)

        @pl.when(f_active & jnp.logical_not(mine))
        def _(where=where):
            push(fst, fin_dst, fs_send, y_sem, at(*where)).start()
            push(fates_st.at[where[2] // 2], fate_dst, fs_send, f_sem, at(*where)).start()

        @pl.when(f_active & mine)
        def _(where=where):
            pltpu.make_async_copy(fst, fin_dst, y_sem).start()
            pltpu.make_async_copy(fates_st.at[where[2] // 2], fate_dst, f_sem).start()

    for k, (cond, where) in enumerate(x_to):
        @pl.when(cond)
        def _(where=where):
            push(xst, xbuf.at[z % 4], in_send, x_sem.at[z % 4], at(*where)).start()

    @pl.when(c == home)
    def _():
        pltpu.make_async_copy(xst, xbuf.at[z % 4], x_sem.at[z % 4]).start()

    live_now = jnp.int32(0)
    live_next = jnp.int32(0)
    for k in range(4):
        live_now = live_now + jnp.where(p == k, live_ref[k], 0)
        live_next = live_next + jnp.where(p == k, live_ref[k + 1], 0)
    log_now = jnp.log2(jnp.broadcast_to(live_now.astype(F32), (8, LANES)))
    log_next = jnp.log2(jnp.broadcast_to(live_next.astype(F32), (8, LANES)))
    lanes, subs = lane_iota(), sub_iota()
    row_ids = [HALF * c + LANES * (8 * r + subs) + lanes for r in range(2)]
    col_ids = QUARTER * b + 8 * lanes + subs
    log_b = jnp.where(col_ids < live_next, -log_next, NEG)

    pltpu.make_async_copy(ybuf, ybuf, y_sem).wait()
    row_of = lax.broadcasted_iota(jnp.int32, (32, 512), 0)
    keep = row_of < 30
    for k in range(2):
        cells = jnp.where(keep, ybuf[k], 0.0)
        norms = jnp.sum(cells * cells, axis=0, keepdims=True)
        for q in range(4):
            flat = jnp.broadcast_to(norms[:, LANES * q : LANES * (q + 1)], (LANES, LANES))
            first = 512 * k + LANES * q
            vb[first : first + LANES, :] = jnp.transpose(flat)
        high, mid, low = three_parts(-2.0 * cells)
        stack = jnp.concatenate([jnp.where(row_of == 30, norms, high), mid, low, high], axis=0)
        yt[512 * k : 512 * (k + 1), :] = jnp.transpose(stack)
    for sub in range(8):
        turned = jnp.transpose(yt[pl.ds(sub, LANES, stride=8), :])
        yk[:, LANES * sub : LANES * (sub + 1)] = turned.astype(BF16)
        ysq[sub : sub + 1, :] = turned[30:31, :]

    def merge(first, second):
        peak = jnp.maximum(first[0], second[0])
        return peak, first[1] * jnp.exp2(first[0] - peak) + second[1] * jnp.exp2(second[0] - peak)

    columns = None
    for r in range(2):
        x_rows = []
        g_rows = []
        for k in range(2 * r, 2 * r + 2):
            block = xbuf.at[k]
            pltpu.make_async_copy(block, block, x_sem.at[k]).wait()
            cells = jnp.where(keep, xbuf[k], 0.0)
            norms = jnp.sum(cells * cells, axis=0, keepdims=True)
            x_rows += [norms[:, LANES * q : LANES * (q + 1)] for q in range(4)]
            g_rows += [xbuf[k, 30:31, LANES * q : LANES * (q + 1)] for q in range(4)]
            high, mid, low = three_parts(cells)
            none = jnp.zeros_like(high)
            for part, stack in enumerate(([high, high, high, none], [mid, mid, none, low])):
                stack = jnp.concatenate(stack, axis=0)
                xk[LANES * part : LANES * (part + 1), 512 * k : 512 * (k + 1)] = stack.astype(BF16)
                turned = jnp.transpose(stack)
                for q in range(4):
                    first = 1024 * r + 4 * (k % 2) + q
                    (xt0, xt1)[part][pl.ds(first, LANES, stride=8), :] = turned[LANES * q : LANES * (q + 1), :]
        grown = jnp.concatenate(g_rows, axis=0)
        log_a = jnp.where(row_ids[r] < live_now, jnp.log2(grown) - log_now, NEG)
        la[r] = log_a
        spread_columns(jnp.concatenate(x_rows, axis=0), ub.at[r])

        def ct_rows(k, carry, r=r, x_rows=x_rows):
            row = pl.multiple_of(k * 256, 256)
            left = yt[pl.ds(row, 256), :].astype(BF16)
            left = jnp.concatenate([left, left], axis=1)
            cross = jnp.dot(left, xk[:, 1024 * r : 1024 * (r + 1)], preferred_element_type=F32)
            for q in range(8):
                norm = vb[pl.ds(row, 256), :] + x_rows[q]
                ct[r, pl.ds(row, 256), LANES * q : LANES * (q + 1)] = (
                    norm + cross[:, LANES * q : LANES * (q + 1)]
                ) * COST_SCALE
            return carry

        lax.fori_loop(0, 4, ct_rows, 0)

        def cr_rows(k, carry, r=r):
            row = pl.multiple_of(k * 256, 256)
            both = pl.multiple_of(1024 * r + k * 256, 256)
            left = jnp.concatenate([xt0[pl.ds(both, 256), :], xt1[pl.ds(both, 256), :]], axis=1).astype(BF16)
            right = yk[...]
            cross = jnp.dot(left, jnp.concatenate([right, right], axis=0), preferred_element_type=F32)
            for q in range(8):
                norm = ub[r, pl.ds(row, 256), :] + ysq[q : q + 1, :]
                cr[r, pl.ds(row, 256), LANES * q : LANES * (q + 1)] = (
                    norm + cross[:, LANES * q : LANES * (q + 1)]
                ) * COST_SCALE
            return carry

        lax.fori_loop(0, 4, cr_rows, 0)
        spread_columns(log_a, ub.at[r])
        found = lse_pass(cr.at[r], ub.at[r])
        columns = found if columns is None else merge(columns, found)

    def from_columns(par, m0, s0):
        csend[par, 0:8] = m0
        csend[par, 8:16] = s0
        copy = push(csend.at[par], cslot.at[par], cs_send.at[par], cs_recv.at[par], at(*core_peer))
        copy.start()
        copy.wait()
        peak, total = merge((m0, s0), (cslot[par, 0:8], cslot[par, 8:16]))
        spread_columns(-SHRINK * (peak + jnp.log2(total)) + log_b, vb)

    def send_rows(par):
        def half(r, carry):
            m, s = lse_pass(ct.at[r], vb)
            rsend[par, r, 0:8] = m
            rsend[par, r, 8:16] = s
            rslot[par, r, b, 0:8] = m
            rslot[par, r, b, 8:16] = s
            for where in row_peers:
                push(
                    rsend.at[par, r], rslot.at[par, r, b], rs_send.at[par, r], rs_recv.at[par, r], at(*where)
                ).start()
            return carry

        lax.fori_loop(0, 2, half, 0)

    def from_rows(par, r):
        three = rslot.at[par, r, pl.ds(0, 3)]
        pltpu.make_async_copy(three, three, rs_recv.at[par, r]).wait()
        pltpu.make_async_copy(three, three, rs_send.at[par, r]).wait()
        ms = [rslot[par, r, k, 0:8] for k in range(4)]
        ss = [rslot[par, r, k, 8:16] for k in range(4)]
        peak = jnp.maximum(jnp.maximum(ms[0], ms[1]), jnp.maximum(ms[2], ms[3]))
        terms = [ss[k] * jnp.exp2(ms[k] - peak) for k in range(4)]
        total = (terms[0] + terms[1]) + (terms[2] + terms[3])
        return peak, total, -SHRINK * (peak + jnp.log2(total))

    def iterate(step, carry):
        par = step % 2
        from_columns(par, *carry)
        send_rows(par)

        def half(r, so_far):
            level = from_rows(par, r)[2]
            spread_columns(level + la[r], ub.at[r])
            return merge(so_far, lse_pass(cr.at[r], ub.at[r]))

        return lax.fori_loop(0, 2, half, (jnp.full((8, LANES), LOWEST, F32), jnp.zeros((8, LANES), F32)))

    columns = lax.fori_loop(0, ITERS - 1, iterate, columns)
    par = (ITERS - 1) % 2
    from_columns(par, *columns)
    send_rows(par)

    for r in range(2):
        wpeak = [rsend[par, r, q : q + 1, :] for q in range(8)]

        def w_rows(k, carry, r=r, wpeak=wpeak):
            for j in range(4):
                row = pl.multiple_of(k * 64 + 16 * j, 16)
                left = vb[pl.ds(row, 16), :]
                for q in range(8):
                    first = 1024 * r + LANES * q
                    s = left - ct[r, pl.ds(row, 16), LANES * q : LANES * (q + 1)]
                    wt[pl.ds(row, 16), first : first + LANES] = jnp.exp2(s - wpeak[q]).astype(BF16)
            return carry

        lax.fori_loop(0, QUARTER // 64, w_rows, 0)

    scales = []
    for r in range(2):
        peak, total, level = from_rows(par, r)
        fsend[8 * r : 8 * r + 8] = level * (EPS / LOG2E)
        scale = jnp.exp2(rsend[par, r, 0:8] - peak) / total
        scale = jnp.where(row_ids[r] < live_now, scale, 0.0)
        scales += [scale[q : q + 1, :] for q in range(8)]

    pot_copy = push(fsend, fother, p_send, p_recv, at(*core_peer))
    pot_copy.start()

    @pl.when(last)
    def _():
        pltpu.make_async_copy(hand, hand, f_sem).wait()

    @pl.when(jnp.logical_not(last))
    def _():
        pltpu.make_async_copy(chin, chin, ch_recv).wait()
        total = chin[0].astype(F32)
        for k in range(1, 4):
            total = total + chin[k].astype(F32)
        hand[...] = total.astype(BF16)

    for r in range(2):
        part = jnp.dot(hand[...], wt[:, 1024 * r : 1024 * (r + 1)], preferred_element_type=F32)
        for q in range(8):
            tile = part[:, LANES * q : LANES * (q + 1)] * scales[8 * r + q]
            pbuf[:, 1024 * r + LANES * q : 1024 * r + LANES * (q + 1)] = tile
            pbf[r, :, LANES * q : LANES * (q + 1)] = tile.astype(BF16)
    for k, (cond, where) in enumerate(ch_to):
        @pl.when(cond)
        def _(k=k, where=where):
            push(pbf.at[k // 2], chin.at[b], ch_send, ch_recv, at(*where)).start()

    def s1_src(k):
        first = pl.multiple_of(QUARTER * (a % 2) + LANES * k, LANES)
        return pbuf.at[:, pl.ds(first, LANES)]

    for k, where in enumerate(s1_to):
        mine = same(*where)

        @pl.when((c == home) & jnp.logical_not(mine))
        def _(k=k, where=where):
            push(s1_src(k), s1.at[b], s1_send, s1_recv, at(*where)).start()

        @pl.when((c == home) & mine)
        def _(k=k):
            pltpu.make_async_copy(s1_src(k), s1.at[b], s1_recv).start()

    pltpu.make_async_copy(s1, s1, s1_recv).wait()
    s2st[...] = (s1[0] + s1[1]) + (s1[2] + s1[3])
    for where in s2_to:
        mine = same(*where)

        @pl.when(jnp.logical_not(mine))
        def _(where=where):
            push(s2st, s2.at[d], s2_send, s2_recv, at(*where)).start()

        @pl.when(mine)
        def _():
            pltpu.make_async_copy(s2st, s2.at[d], s2_recv).start()

    pot_copy.wait()
    own = jnp.where(c == home, fsend[...], fother[...])
    picked = own[0:4]
    for k in range(1, 4):
        picked = jnp.where(z % 4 == k, own[4 * k : 4 * k + 4], picked)
    for k in range(4):
        pot_ref[0:1, LANES * k : LANES * (k + 1)] = picked[k : k + 1]

    pltpu.make_async_copy(s2, s2, s2_recv).wait()
    turn = lax.rem(LANES - 32 * quad, LANES)
    for g in range(4):
        out_ref[0, 10 * g : 10 * g + 10, :] = pltpu.roll(s2[g], turn, axis=1)[0:10, 0:32]

    def settle(cond, ref, sem):
        @pl.when(cond)
        def _():
            pltpu.make_async_copy(ref, ref, sem).wait()

    for cond, where in x_to + y_to:
        settle(cond, xst, in_send)
    for where in f_to:
        off = f_active & jnp.logical_not(same(*where))
        settle(off, fst, fs_send)
        settle(off, fates_st.at[0], fs_send)
    for cond, where in ch_to:
        settle(cond, pbf.at[0], ch_send)
    for where in s1_to:
        settle((c == home) & jnp.logical_not(same(*where)), s2st, s1_send)
    for where in s2_to:
        settle(jnp.logical_not(same(*where)), s2st, s2_send)


def local(src_cells, final_cells, growth, live, final_fates):
    vmem = pl.BlockSpec(memory_space=pltpu.VMEM)
    dma = pltpu.SemaphoreType.DMA
    V = pltpu.VMEM
    return tuple(pl.pallas_call(
        kernel,
        out_shape=(
            jax.ShapeDtypeStruct((1, 40, 32), F32),
            jax.ShapeDtypeStruct((1, 512), F32),
        ),
        in_specs=[vmem, vmem, vmem, pl.BlockSpec(memory_space=pltpu.SMEM), vmem],
        out_specs=(vmem, vmem),
        scratch_shapes=[
            V((32, 512), F32), V((32, 256), F32), V((4, 16, 256), BF16),
            V((4, 32, 512), F32), V((2, 32, 512), F32),
            V((256, HALF), BF16), V((HALF, 128), F32), V((HALF, 128), F32), V((QUARTER, 128), F32), V((128, QUARTER), BF16),
            V((8, 128), F32), V((2, 8, 128), F32),
            V((2, QUARTER, QUARTER), F32), V((2, QUARTER, QUARTER), F32),
            V((2, QUARTER, 128), F32), V((QUARTER, 128), F32), V((QUARTER, HALF), BF16),
            V((2, 16, 128), F32), V((2, 16, 128), F32), V((2, 2, 16, 128), F32), V((2, 2, 4, 16, 128), F32),
            V((16, 128), F32), V((16, 128), F32),
            V((16, QUARTER), BF16), V((16, HALF), F32), V((2, 16, QUARTER), BF16), V((4, 16, QUARTER), BF16),
            V((4, 16, 128), F32), V((16, 128), F32), V((4, 16, 128), F32),
            dma(()), dma((4,)), dma(()), dma(()), dma(()), dma((2,)), dma((2,)), dma((2, 2)), dma((2, 2)),
            dma(()), dma(()), dma(()), dma(()), dma(()), dma(()), dma(()), dma(()),
        ],
        compiler_params=pltpu.CompilerParams(
            collective_id=0, has_side_effects=True, vmem_limit_bytes=48 * 2**20
        ),
        name="transport",
    )(src_cells, final_cells, growth, live, final_fates))


def solution(mesh):
    placed = (P("pair", None, "src"), P(None, "tgt"), P("pair", "src"), P(), P(None, "tgt"))
    return jax.shard_map(
        local,
        mesh=mesh,
        in_specs=placed,
        out_specs=(P("pair", None, ("src", "tgt")), P("pair", "src")),
        check_vma=False,
    )
```

```python
import functools
import math

import jax
import jax.numpy as jnp
from jax import lax
from jax.experimental import pallas as pl
from jax.experimental.pallas import tpu as pltpu
from jax.sharding import PartitionSpec as P

MESH = pl.DeviceIdType.MESH
F32 = jnp.float32
BF16 = jnp.bfloat16

ITERS = 8
EPS = 0.1
LAM = 1.0
NEG = -1e30
SHRINK = LAM / (LAM + EPS)
LOG2E = 1.0 / math.log(2.0)
COST_SCALE = LOG2E / (EPS * 60.0)
LOWEST = -3e38

HALF = 2048
QUARTER = 1024
LANES = 128
GROUP = 32


def lane_iota():
    return lax.broadcasted_iota(jnp.int32, (8, LANES), 1)


def sub_iota():
    return lax.broadcasted_iota(jnp.int32, (8, LANES), 0)


def spread_columns(packed, dst):
    for t in range(LANES):
        dst[8 * t : 8 * t + 8, :] = jnp.broadcast_to(packed[:, t : t + 1], (8, LANES))


def lse_pass(cost, spread):
    tiles = 8
    rows = 8 * GROUP

    def walk(start, update):
        def body(k, acc):
            acc = list(acc)
            first = pl.multiple_of(k * rows, rows)
            left_rows = spread.at[pl.ds(first, rows)]
            cost_rows = cost.at[pl.ds(first, rows)]
            for t in range(GROUP):
                left = left_rows[8 * t : 8 * t + 8, :]
                for q in range(tiles):
                    acc[q] = update(q, acc[q], left - cost_rows[8 * t : 8 * t + 8, LANES * q : LANES * (q + 1)])
            return tuple(acc)

        return lax.fori_loop(0, QUARTER // rows, body, tuple(start))

    peaks = walk([jnp.full((8, LANES), LOWEST, F32)] * tiles, lambda q, a, s: jnp.maximum(a, s))
    peaks = [jnp.broadcast_to(jnp.max(a, axis=0, keepdims=True), (8, LANES)) for a in peaks]
    sums = walk([jnp.zeros((8, LANES), F32)] * tiles, lambda q, a, s: a + jnp.exp2(s - peaks[q]))
    sums = [jnp.broadcast_to(jnp.sum(a, axis=0, keepdims=True), (8, LANES)) for a in sums]
    which = sub_iota()
    m, s = peaks[0], sums[0]
    for q in range(1, 8):
        m = jnp.where(which == q, peaks[q], m)
        s = jnp.where(which == q, sums[q], s)
    return m, s


def three_parts(x):
    high = x.astype(BF16).astype(F32)
    rest = x - high
    mid = rest.astype(BF16).astype(F32)
    low = (rest - mid).astype(BF16).astype(F32)
    return high, mid, low


def kernel(
    src_ref, fin_ref, growth_ref, live_ref, fates_ref, out_ref, pot_ref,
    xst, fst, fates_st, xbuf, ybuf, xk, xt0, xt1, yt, yk, ysq, la, ct, cr, ub, vb, wt,
    csend, cslot, rsend, rslot, fsend, fother, hand, pbuf, pbf, chin, s2,
    in_send, x_sem, y_sem, f_sem, fs_send, cs_send, cs_recv, rs_send, rs_recv,
    p_send, p_recv, ch_send, ch_recv, yf_send, yf_recv, s2_send, s2_recv, hx_send, hx_recv,
):
    p = lax.axis_index("pair")
    z = lax.axis_index("src")
    t = lax.axis_index("tgt")
    y, c = t // 2, t % 2
    zb, yb = z % 2, y % 2
    b = 2 * zb + yb
    z0, y0 = z - zb, y - yb
    a, d = z // 2, y // 2
    home = z // 4
    last = p == 3

    def at(pp, zz, yy, cc):
        return {"pair": pp, "src": zz, "tgt": 2 * yy + cc}

    def push(src, dst, send, recv, where):
        return pltpu.make_async_remote_copy(src, dst, send, recv, device_id=where, device_id_type=MESH)

    def same(pp, zz, yy, cc):
        return (pp == p) & (zz == z) & (yy == y) & (cc == c)

    up, down = jnp.minimum(p + 1, 3), jnp.maximum(p - 1, 0)
    chips = [((b + k) % 4) for k in range(1, 4)]
    chip_at = lambda bb: (z0 + bb // 2, y0 + bb % 2)
    core_peer = (p, z, y, 1 - c)
    row_peers = [(p, *chip_at(bb), c) for bb in chips]
    x_to = [(c == home, (p, (z + k) % 8, y, c)) for k in range(1, 8)]
    x_from = [(4 * c + k != z, (p, 4 * c + k, y, c)) for k in range(4)]
    y_active = (p > 0) & (yb == a % 2)
    y_to = [(y_active, (down, home + 2 * k, y, c)) for k in range(4)]
    y_from = [(p < 3, (up, 2 * b + k, y, c)) for k in range(2)]
    f_active = last & (zb == y // 4)
    f_to = [(p, z, d % 2 + 2 * (k // 2), k % 2) for k in range(8)]
    f_from = [(p, z, 2 * b + k // 2, k % 2) for k in range(4)]
    ch_to = [(p > 0, (down, *chip_at(2 * c + k // 2), k % 2)) for k in range(4)]
    ch_from = [(p < 3, (up, *chip_at(k), b // 2)) for k in range(4)]
    quad = 2 * yb + c

    def out_to(k):
        return p, z0 + k // 16, 2 * (k // 4 % 4) + k // 2 % 2, k % 2

    def out_from(k):
        return p, z0 + k // 8, 2 * (k // 2 % 4) + k % 2, home

    barrier = pltpu.get_barrier_semaphore()
    expected = jnp.int32(4)

    def greet(cond, where):
        @pl.when(cond)
        def _():
            pl.semaphore_signal(barrier, inc=1, device_id=at(*where), device_id_type=MESH)

    pl.semaphore_signal(barrier, inc=1, device_id=at(*core_peer), device_id_type=MESH)
    for where in row_peers:
        pl.semaphore_signal(barrier, inc=1, device_id=at(*where), device_id_type=MESH)
    for cond, where in x_from + y_from + ch_from:
        greet(cond, where)
    for where in f_from:
        greet(last & jnp.logical_not(same(*where)), where)
    for k in range(16):
        greet(jnp.logical_not(same(*out_from(k))), out_from(k))
    for cond, where in x_to + y_to + ch_to:
        expected = expected + jnp.where(cond, 1, 0)
    for where in f_to:
        expected = expected + jnp.where(f_active & jnp.logical_not(same(*where)), 1, 0)
    expected = expected + jnp.where(c == home, 31, 0)

    xst[30:32, :] = jnp.zeros((2, 512), F32)
    xst[0:30, :] = src_ref[:, 0, :]
    xst[30:31, :] = growth_ref[...]
    fst[...] = jnp.zeros_like(fst)
    fst[0:30, :] = fin_ref[...]
    for g in range(4):
        block = jnp.concatenate([fates_ref[10 * g : 10 * g + 10, :], jnp.zeros((6, 256), F32)], axis=0)
        fates_st[g] = block.astype(BF16)

    pl.semaphore_wait(barrier, expected)

    def my_lanes(ref):
        first = pl.multiple_of(256 * c, 256)
        return ref.at[:, pl.ds(first, 256)]

    for cond, where in y_to:
        @pl.when(cond)
        def _(where=where):
            push(my_lanes(xst), my_lanes(ybuf.at[zb]), in_send, y_sem, at(*where)).start()

    slot = t % 4
    fin_dst = ybuf.at[slot // 2, :, pl.ds(pl.multiple_of((slot % 2) * 256, 256), 256)]
    fate_dst = hand.at[slot // 2, :, pl.ds(pl.multiple_of((slot % 2) * 256, 256), 256)]
    for where in f_to:
        mine = same(*where)

        @pl.when(f_active & jnp.logical_not(mine) & (where[3] == c))
        def _(where=where):
            push(fst, fin_dst, fs_send, y_sem, at(*where)).start()

        @pl.when(f_active & jnp.logical_not(mine))
        def _(where=where):
            push(fates_st.at[where[2] // 2], fate_dst, fs_send, f_sem, at(*where)).start()

        @pl.when(f_active & mine)
        def _(where=where):
            pltpu.make_async_copy(fst, fin_dst, y_sem).start()
            pltpu.make_async_copy(fates_st.at[where[2] // 2], fate_dst, f_sem).start()

    def send_cells(chosen):
        for cond, where in x_to:
            @pl.when(cond & chosen)
            def _(where=where):
                push(xst, xbuf.at[z % 4], in_send, x_sem.at[z % 4], at(*where)).start()

        @pl.when((c == home) & chosen)
        def _():
            pltpu.make_async_copy(xst, xbuf.at[z % 4], x_sem.at[z % 4]).start()

    send_cells(z % 4 < 2)

    live_now = jnp.int32(0)
    live_next = jnp.int32(0)
    for k in range(4):
        live_now = live_now + jnp.where(p == k, live_ref[k], 0)
        live_next = live_next + jnp.where(p == k, live_ref[k + 1], 0)
    log_now = jnp.log2(jnp.broadcast_to(live_now.astype(F32), (8, LANES)))
    log_next = jnp.log2(jnp.broadcast_to(live_next.astype(F32), (8, LANES)))
    lanes, subs = lane_iota(), sub_iota()
    row_ids = [HALF * c + LANES * (8 * r + subs) + lanes for r in range(2)]
    col_ids = QUARTER * b + 8 * lanes + subs
    log_b = jnp.where(col_ids < live_next, -log_next, NEG)

    half = ybuf.at[:, :, pl.ds(0, 256)]
    pltpu.make_async_copy(half, half, y_sem).wait()
    mine = ybuf.at[:, :, pl.ds(pl.multiple_of(256 * c, 256), 256)]
    y_copy = push(mine, mine, yf_send, yf_recv, at(*core_peer))
    y_copy.start()
    send_cells(z % 4 >= 2)
    y_copy.wait()
    row_of = lax.broadcasted_iota(jnp.int32, (32, 512), 0)
    keep = row_of < 30
    for k in range(2):
        cells = jnp.where(keep, ybuf[k], 0.0)
        norms = jnp.sum(cells * cells, axis=0, keepdims=True)
        for q in range(4):
            flat = jnp.broadcast_to(norms[:, LANES * q : LANES * (q + 1)], (LANES, LANES))
            first = 512 * k + LANES * q
            vb[first : first + LANES, :] = jnp.transpose(flat)
        high, mid, low = three_parts(-2.0 * cells)
        stack = jnp.concatenate([jnp.where(row_of == 30, norms, high), mid, low, high], axis=0)
        yt[512 * k : 512 * (k + 1), :] = jnp.transpose(stack)
    for sub in range(8):
        turned = jnp.transpose(yt[pl.ds(sub, LANES, stride=8), :])
        yk[:, LANES * sub : LANES * (sub + 1)] = turned.astype(BF16)
        ysq[sub : sub + 1, :] = turned[30:31, :]

    def merge(first, second):
        peak = jnp.maximum(first[0], second[0])
        return peak, first[1] * jnp.exp2(first[0] - peak) + second[1] * jnp.exp2(second[0] - peak)

    columns = None
    for r in range(2):
        x_rows = []
        g_rows = []
        for k in range(2 * r, 2 * r + 2):
            block = xbuf.at[k]
            pltpu.make_async_copy(block, block, x_sem.at[k]).wait()
            cells = jnp.where(keep, xbuf[k], 0.0)
            norms = jnp.sum(cells * cells, axis=0, keepdims=True)
            x_rows += [norms[:, LANES * q : LANES * (q + 1)] for q in range(4)]
            g_rows += [xbuf[k, 30:31, LANES * q : LANES * (q + 1)] for q in range(4)]
            high, mid, low = three_parts(cells)
            none = jnp.zeros_like(high)
            for part, stack in enumerate(([high, high, high, none], [mid, mid, none, low])):
                stack = jnp.concatenate(stack, axis=0)
                xk[LANES * part : LANES * (part + 1), 512 * k : 512 * (k + 1)] = stack.astype(BF16)
                turned = jnp.transpose(stack)
                for q in range(4):
                    first = 1024 * r + 4 * (k % 2) + q
                    (xt0, xt1)[part][pl.ds(first, LANES, stride=8), :] = turned[LANES * q : LANES * (q + 1), :]
        grown = jnp.concatenate(g_rows, axis=0)
        log_a = jnp.where(row_ids[r] < live_now, jnp.log2(grown) - log_now, NEG)
        la[r] = log_a
        spread_columns(jnp.concatenate(x_rows, axis=0), ub.at[r])

        def ct_rows(k, carry, r=r, x_rows=x_rows):
            row = pl.multiple_of(k * 256, 256)
            left = yt[pl.ds(row, 256), :].astype(BF16)
            left = jnp.concatenate([left, left], axis=1)
            cross = jnp.dot(left, xk[:, 1024 * r : 1024 * (r + 1)], preferred_element_type=F32)
            for q in range(8):
                norm = vb[pl.ds(row, 256), :] + x_rows[q]
                ct[r, pl.ds(row, 256), LANES * q : LANES * (q + 1)] = (
                    norm + cross[:, LANES * q : LANES * (q + 1)]
                ) * COST_SCALE
            return carry

        lax.fori_loop(0, 4, ct_rows, 0)

        def cr_rows(k, carry, r=r):
            row = pl.multiple_of(k * 256, 256)
            both = pl.multiple_of(1024 * r + k * 256, 256)
            left = jnp.concatenate([xt0[pl.ds(both, 256), :], xt1[pl.ds(both, 256), :]], axis=1).astype(BF16)
            right = yk[...]
            cross = jnp.dot(left, jnp.concatenate([right, right], axis=0), preferred_element_type=F32)
            for q in range(8):
                norm = ub[r, pl.ds(row, 256), :] + ysq[q : q + 1, :]
                cr[r, pl.ds(row, 256), LANES * q : LANES * (q + 1)] = (
                    norm + cross[:, LANES * q : LANES * (q + 1)]
                ) * COST_SCALE
            return carry

        lax.fori_loop(0, 4, cr_rows, 0)
        spread_columns(log_a, ub.at[r])
        found = lse_pass(cr.at[r], ub.at[r])
        columns = found if columns is None else merge(columns, found)

    def from_columns(par, m0, s0):
        csend[par, 0:8] = m0
        csend[par, 8:16] = s0
        copy = push(csend.at[par], cslot.at[par], cs_send.at[par], cs_recv.at[par], at(*core_peer))
        copy.start()
        copy.wait()
        peak, total = merge((m0, s0), (cslot[par, 0:8], cslot[par, 8:16]))
        spread_columns(-SHRINK * (peak + jnp.log2(total)) + log_b, vb)

    def send_rows(par):
        def half(r, carry):
            m, s = lse_pass(ct.at[r], vb)
            rsend[par, r, 0:8] = m
            rsend[par, r, 8:16] = s
            rslot[par, r, b, 0:8] = m
            rslot[par, r, b, 8:16] = s
            for where in row_peers:
                push(
                    rsend.at[par, r], rslot.at[par, r, b], rs_send.at[par, r], rs_recv.at[par, r], at(*where)
                ).start()
            return carry

        lax.fori_loop(0, 2, half, 0)

    def from_rows(par, r):
        three = rslot.at[par, r, pl.ds(0, 3)]
        pltpu.make_async_copy(three, three, rs_recv.at[par, r]).wait()
        pltpu.make_async_copy(three, three, rs_send.at[par, r]).wait()
        ms = [rslot[par, r, k, 0:8] for k in range(4)]
        ss = [rslot[par, r, k, 8:16] for k in range(4)]
        peak = jnp.maximum(jnp.maximum(ms[0], ms[1]), jnp.maximum(ms[2], ms[3]))
        terms = [ss[k] * jnp.exp2(ms[k] - peak) for k in range(4)]
        total = (terms[0] + terms[1]) + (terms[2] + terms[3])
        return peak, total, -SHRINK * (peak + jnp.log2(total))

    def iterate(step, carry):
        par = step % 2
        from_columns(par, *carry)
        send_rows(par)

        def half(r, so_far):
            level = from_rows(par, r)[2]
            spread_columns(level + la[r], ub.at[r])
            return merge(so_far, lse_pass(cr.at[r], ub.at[r]))

        return lax.fori_loop(0, 2, half, (jnp.full((8, LANES), LOWEST, F32), jnp.zeros((8, LANES), F32)))

    columns = lax.fori_loop(0, ITERS - 1, iterate, columns)
    par = (ITERS - 1) % 2
    from_columns(par, *columns)
    send_rows(par)

    for r in range(2):
        wpeak = [rsend[par, r, q : q + 1, :] for q in range(8)]

        def w_rows(k, carry, r=r, wpeak=wpeak):
            for j in range(4):
                row = pl.multiple_of(k * 64 + 16 * j, 16)
                left = vb[pl.ds(row, 16), :]
                for q in range(8):
                    s = left - ct[r, pl.ds(row, 16), LANES * q : LANES * (q + 1)]
                    cr[r, pl.ds(row, 16), LANES * q : LANES * (q + 1)] = jnp.exp2(s - wpeak[q])
            return carry

        lax.fori_loop(0, QUARTER // 64, w_rows, 0)

    for r in range(2):
        peak, total, level = from_rows(par, r)
        fsend[8 * r : 8 * r + 8] = level * (EPS / LOG2E)
        scale = jnp.exp2(rsend[par, r, 0:8] - peak) / total
        scale = jnp.where(row_ids[r] < live_now, scale, 0.0)
        scales = [scale[q : q + 1, :] for q in range(8)]

        def round_rows(k, carry, r=r, scales=scales):
            for j in range(4):
                row = pl.multiple_of(k * 64 + 16 * j, 16)
                for q in range(8):
                    first = 1024 * r + LANES * q
                    w = cr[r, pl.ds(row, 16), LANES * q : LANES * (q + 1)] * scales[q]
                    wt[pl.ds(row, 16), first : first + LANES] = w.astype(BF16)
            return carry

        lax.fori_loop(0, QUARTER // 64, round_rows, 0)


    pot_copy = push(fsend, fother, p_send, p_recv, at(*core_peer))
    pot_copy.start()

    @pl.when(last)
    def _():
        pltpu.make_async_copy(hand, hand, f_sem).wait()

    @pl.when(jnp.logical_not(last))
    def _():
        pltpu.make_async_copy(chin, chin, ch_recv).wait()
        total = (chin[0] + chin[1]) + (chin[2] + chin[3])
        none = jnp.zeros((6, LANES), F32)
        for q in range(4):
            most = total[:, LANES * q : LANES * (q + 1)]
            tile = jnp.concatenate([most, total[2 * q : 2 * q + 2, 512:640], none], axis=0)
            hand[c, :, LANES * q : LANES * (q + 1)] = tile.astype(BF16)
        copy = push(hand.at[c], hand.at[c], hx_send, hx_recv, at(*core_peer))
        copy.start()
        copy.wait()

    handed = jnp.concatenate([hand[0], hand[1]], axis=1)
    for r in range(2):
        tiles = []
        part = jnp.dot(handed, wt[:, 1024 * r : 1024 * (r + 1)], preferred_element_type=F32)
        for q in range(8):
            tile = part[:, LANES * q : LANES * (q + 1)]
            pbuf[8 * r + q] = tile
            tiles.append(tile)
        for h in range(2):
            for q in range(4):
                pbf[r, h, :, LANES * q : LANES * (q + 1)] = tiles[4 * h + q][0:8]
            pbf[r, h, :, 512:640] = jnp.concatenate([tiles[4 * h + q][8:10] for q in range(4)], axis=0)
    for k, (cond, where) in enumerate(ch_to):
        @pl.when(cond)
        def _(k=k, where=where):
            push(pbf.at[k // 2, k % 2], chin.at[b], ch_send, ch_recv, at(*where)).start()

    @pl.when(c == home)
    def _():
        def send_out(k, carry):
            where = out_to(k)
            tile = pbuf.at[8 * (a % 2) + k // 4]
            mine = same(*where)

            @pl.when(jnp.logical_not(mine))
            def _():
                push(tile, s2.at[d, b], s2_send, s2_recv, at(*where)).start()

            @pl.when(mine)
            def _():
                pltpu.make_async_copy(tile, s2.at[d, b], s2_recv).start()

            return carry

        lax.fori_loop(0, 32, send_out, 0)

    pot_copy.wait()
    own = jnp.where(c == home, fsend[...], fother[...])
    picked = own[0:4]
    for k in range(1, 4):
        picked = jnp.where(z % 4 == k, own[4 * k : 4 * k + 4], picked)
    for k in range(4):
        pot_ref[0:1, LANES * k : LANES * (k + 1)] = picked[k : k + 1]

    pltpu.make_async_copy(s2, s2, s2_recv).wait()
    turn = lax.rem(LANES - 32 * quad, LANES)
    for g in range(4):
        four = [s2[g, k] for k in range(4)]
        tile = (four[0] + four[1]) + (four[2] + four[3])
        out_ref[0, 10 * g : 10 * g + 10, :] = pltpu.roll(tile, turn, axis=1)[0:10, 0:32]

    def settle(cond, ref, sem):
        @pl.when(cond)
        def _():
            pltpu.make_async_copy(ref, ref, sem).wait()

    for cond, where in x_to:
        settle(cond, xst, in_send)
    for cond, where in y_to:
        settle(cond, fst, in_send)
    for where in f_to:
        off = f_active & jnp.logical_not(same(*where))
        settle(off & (where[3] == c), fst, fs_send)
        settle(off, fates_st.at[0], fs_send)
    for cond, where in ch_to:
        settle(cond, pbf.at[0, 0], ch_send)
    settle(c == home, pbuf, s2_send)
    settle(c == home, pbuf.at[pl.ds(0, 15)], s2_send)


def local(src_cells, final_cells, growth, live, final_fates):
    vmem = pl.BlockSpec(memory_space=pltpu.VMEM)
    dma = pltpu.SemaphoreType.DMA
    V = pltpu.VMEM
    return tuple(pl.pallas_call(
        kernel,
        out_shape=(
            jax.ShapeDtypeStruct((1, 40, 32), F32),
            jax.ShapeDtypeStruct((1, 512), F32),
        ),
        in_specs=[vmem, vmem, vmem, pl.BlockSpec(memory_space=pltpu.SMEM), vmem],
        out_specs=(vmem, vmem),
        scratch_shapes=[
            V((32, 512), F32), V((32, 256), F32), V((4, 16, 256), BF16),
            V((4, 32, 512), F32), V((2, 32, 512), F32),
            V((256, HALF), BF16), V((HALF, 128), F32), V((HALF, 128), F32), V((QUARTER, 128), F32), V((128, QUARTER), BF16),
            V((8, 128), F32), V((2, 8, 128), F32),
            V((2, QUARTER, QUARTER), F32), V((2, QUARTER, QUARTER), F32),
            V((2, QUARTER, 128), F32), V((QUARTER, 128), F32), V((QUARTER, HALF), BF16),
            V((2, 16, 128), F32), V((2, 16, 128), F32), V((2, 2, 16, 128), F32), V((2, 2, 4, 16, 128), F32),
            V((16, 128), F32), V((16, 128), F32),
            V((2, 16, 512), BF16), V((16, 16, 128), F32), V((2, 2, 8, 640), F32), V((4, 8, 640), F32),
            V((4, 4, 16, 128), F32),
            dma(()), dma((4,)), dma(()), dma(()), dma(()), dma((2,)), dma((2,)), dma((2, 2)), dma((2, 2)),
            dma(()), dma(()), dma(()), dma(()), dma(()), dma(()), dma(()), dma(()), dma(()), dma(()),
        ],
        compiler_params=pltpu.CompilerParams(
            collective_id=0, has_side_effects=True, vmem_limit_bytes=48 * 2**20
        ),
        name="transport",
    )(jnp.transpose(src_cells, (1, 0, 2)), final_cells, growth, live, final_fates))


def solution(mesh):
    placed = (P("pair", None, "src"), P(None, "tgt"), P("pair", "src"), P(), P(None, "tgt"))
    return jax.shard_map(
        local,
        mesh=mesh,
        in_specs=placed,
        out_specs=(P("pair", None, ("src", "tgt")), P("pair", "src")),
        check_vma=False,
    )
```

```python
import functools
import math

import jax
import jax.numpy as jnp
from jax import lax
from jax.experimental import pallas as pl
from jax.experimental.pallas import tpu as pltpu
from jax.sharding import PartitionSpec as P

MESH = pl.DeviceIdType.MESH
F32 = jnp.float32
BF16 = jnp.bfloat16

ITERS = 8
EPS = 0.1
LAM = 1.0
NEG = -1e30
SHRINK = LAM / (LAM + EPS)
LOG2E = 1.0 / math.log(2.0)
COST_SCALE = LOG2E / (EPS * 60.0)
LOWEST = -3e38

HALF = 2048
QUARTER = 1024
LANES = 128
GROUP = 64


def lane_iota():
    return lax.broadcasted_iota(jnp.int32, (8, LANES), 1)


def sub_iota():
    return lax.broadcasted_iota(jnp.int32, (8, LANES), 0)


def spread_columns(packed, dst):
    for t in range(LANES):
        dst[8 * t : 8 * t + 8, :] = jnp.broadcast_to(packed[:, t : t + 1], (8, LANES))


def lse_pass(cost, spread):
    tiles = 8
    rows = 8 * GROUP

    def walk(start, update):
        def body(k, acc):
            acc = list(acc)
            first = pl.multiple_of(k * rows, rows)
            left_rows = spread.at[pl.ds(first, rows)]
            cost_rows = cost.at[pl.ds(first, rows)]
            for t in range(GROUP):
                left = left_rows[8 * t : 8 * t + 8, :]
                for q in range(tiles):
                    acc[q] = update(q, acc[q], left - cost_rows[8 * t : 8 * t + 8, LANES * q : LANES * (q + 1)])
            return tuple(acc)

        return lax.fori_loop(0, QUARTER // rows, body, tuple(start))

    peaks = walk([jnp.full((8, LANES), LOWEST, F32)] * tiles, lambda q, a, s: jnp.maximum(a, s))
    peaks = [jnp.broadcast_to(jnp.max(a, axis=0, keepdims=True), (8, LANES)) for a in peaks]
    sums = walk([jnp.zeros((8, LANES), F32)] * tiles, lambda q, a, s: a + jnp.exp2(s - peaks[q]))
    sums = [jnp.broadcast_to(jnp.sum(a, axis=0, keepdims=True), (8, LANES)) for a in sums]
    which = sub_iota()
    m, s = peaks[0], sums[0]
    for q in range(1, 8):
        m = jnp.where(which == q, peaks[q], m)
        s = jnp.where(which == q, sums[q], s)
    return m, s


def three_parts(x):
    high = x.astype(BF16).astype(F32)
    rest = x - high
    mid = rest.astype(BF16).astype(F32)
    low = (rest - mid).astype(BF16).astype(F32)
    return high, mid, low


def kernel(
    src_ref, fin_ref, growth_ref, live_ref, fates_ref, out_ref, pot_ref,
    xst, fst, fates_st, xbuf, ybuf, xk, xt0, xt1, yt, yk, ysq, la, ct, cr, ub, vb, wt,
    csend, cslot, rsend, rslot, fsend, fother, hand, pbuf, pbf, chin, s2,
    in_send, x_sem, y_sem, f_sem, fs_send, cs_send, cs_recv, rs_send, rs_recv,
    p_send, p_recv, ch_send, ch_recv, yf_send, yf_recv, s2_send, s2_recv, hx_send, hx_recv,
):
    p = lax.axis_index("pair")
    z = lax.axis_index("src")
    t = lax.axis_index("tgt")
    y, c = t // 2, t % 2
    zb, yb = z % 2, y % 2
    b = 2 * zb + yb
    z0, y0 = z - zb, y - yb
    a, d = z // 2, y // 2
    home = z // 4
    last = p == 3

    def at(pp, zz, yy, cc):
        return {"pair": pp, "src": zz, "tgt": 2 * yy + cc}

    def push(src, dst, send, recv, where):
        return pltpu.make_async_remote_copy(src, dst, send, recv, device_id=where, device_id_type=MESH)

    def same(pp, zz, yy, cc):
        return (pp == p) & (zz == z) & (yy == y) & (cc == c)

    up, down = jnp.minimum(p + 1, 3), jnp.maximum(p - 1, 0)
    chips = [3 - b, (b + 2) % 4, b + 1 - 2 * (b % 2)]
    chip_at = lambda bb: (z0 + bb // 2, y0 + bb % 2)
    core_peer = (p, z, y, 1 - c)
    row_peers = [(p, *chip_at(bb), c) for bb in chips]
    x_to = [(c == home, (p, (z + k) % 8, y, c)) for k in (4, 3, 5, 2, 6, 1, 7)]
    x_from = [(4 * c + k != z, (p, 4 * c + k, y, c)) for k in range(4)]
    y_active = (p > 0) & (yb == a % 2)
    y_to = [(y_active, (down, home + 2 * k, y, c)) for k in range(4)]
    y_from = [(p < 3, (up, 2 * b + k, y, c)) for k in range(2)]
    f_active = last & (zb == y // 4)
    f_to = [(p, z, d % 2 + 2 * (k // 2), k % 2) for k in range(8)]
    f_from = [(p, z, 2 * b + k // 2, k % 2) for k in range(4)]
    ch_to = [(p > 0, (down, *chip_at(2 * c + k // 2), k % 2)) for k in range(4)]
    ch_from = [(p < 3, (up, *chip_at(k), b // 2)) for k in range(4)]
    quad = 2 * yb + c

    def out_to(k):
        return p, z0 + k // 16, 2 * (k // 4 % 4) + k // 2 % 2, k % 2

    def out_from(k):
        return p, z0 + k // 8, 2 * (k // 2 % 4) + k % 2, home

    barrier = pltpu.get_barrier_semaphore()
    expected = jnp.int32(4)

    def greet(cond, where):
        @pl.when(cond)
        def _():
            pl.semaphore_signal(barrier, inc=1, device_id=at(*where), device_id_type=MESH)

    pl.semaphore_signal(barrier, inc=1, device_id=at(*core_peer), device_id_type=MESH)
    for where in row_peers:
        pl.semaphore_signal(barrier, inc=1, device_id=at(*where), device_id_type=MESH)
    for cond, where in x_from + y_from + ch_from:
        greet(cond, where)
    for where in f_from:
        greet(last & jnp.logical_not(same(*where)), where)
    for k in range(16):
        greet(jnp.logical_not(same(*out_from(k))), out_from(k))
    for cond, where in x_to + y_to + ch_to:
        expected = expected + jnp.where(cond, 1, 0)
    for where in f_to:
        expected = expected + jnp.where(f_active & jnp.logical_not(same(*where)), 1, 0)
    expected = expected + jnp.where(c == home, 31, 0)

    xst[30:32, :] = jnp.zeros((2, 512), F32)
    xst[0:30, :] = src_ref[:, 0, :]
    xst[30:31, :] = growth_ref[...]
    fst[...] = jnp.zeros_like(fst)
    fst[0:30, :] = fin_ref[...]
    for g in range(4):
        block = jnp.concatenate([fates_ref[10 * g : 10 * g + 10, :], jnp.zeros((6, 256), F32)], axis=0)
        fates_st[g] = block.astype(BF16)

    pl.semaphore_wait(barrier, expected)

    def my_lanes(ref):
        first = pl.multiple_of(256 * c, 256)
        return ref.at[:, pl.ds(first, 256)]

    for cond, where in y_to:
        @pl.when(cond)
        def _(where=where):
            push(my_lanes(xst), my_lanes(ybuf.at[zb]), in_send, y_sem, at(*where)).start()

    slot = t % 4
    fin_dst = ybuf.at[slot // 2, :, pl.ds(pl.multiple_of((slot % 2) * 256, 256), 256)]
    fate_dst = hand.at[slot // 2, :, pl.ds(pl.multiple_of((slot % 2) * 256, 256), 256)]
    for where in f_to:
        mine = same(*where)

        @pl.when(f_active & jnp.logical_not(mine) & (where[3] == c))
        def _(where=where):
            push(fst, fin_dst, fs_send, y_sem, at(*where)).start()

        @pl.when(f_active & jnp.logical_not(mine))
        def _(where=where):
            push(fates_st.at[where[2] // 2], fate_dst, fs_send, f_sem, at(*where)).start()

        @pl.when(f_active & mine)
        def _(where=where):
            pltpu.make_async_copy(fst, fin_dst, y_sem).start()
            pltpu.make_async_copy(fates_st.at[where[2] // 2], fate_dst, f_sem).start()

    def send_cells(chosen):
        for cond, where in x_to:
            @pl.when(cond & chosen)
            def _(where=where):
                push(xst, xbuf.at[z % 4], in_send, x_sem.at[z % 4], at(*where)).start()

        @pl.when((c == home) & chosen)
        def _():
            pltpu.make_async_copy(xst, xbuf.at[z % 4], x_sem.at[z % 4]).start()

    send_cells(z % 4 < 2)

    live_now = jnp.int32(0)
    live_next = jnp.int32(0)
    for k in range(4):
        live_now = live_now + jnp.where(p == k, live_ref[k], 0)
        live_next = live_next + jnp.where(p == k, live_ref[k + 1], 0)
    log_now = jnp.log2(jnp.broadcast_to(live_now.astype(F32), (8, LANES)))
    log_next = jnp.log2(jnp.broadcast_to(live_next.astype(F32), (8, LANES)))
    lanes, subs = lane_iota(), sub_iota()
    row_ids = [HALF * c + LANES * (8 * r + subs) + lanes for r in range(2)]
    col_ids = QUARTER * b + 8 * lanes + subs
    log_b = jnp.where(col_ids < live_next, -log_next, NEG)

    half = ybuf.at[:, :, pl.ds(0, 256)]
    pltpu.make_async_copy(half, half, y_sem).wait()
    mine = ybuf.at[:, :, pl.ds(pl.multiple_of(256 * c, 256), 256)]
    y_copy = push(mine, mine, yf_send, yf_recv, at(*core_peer))
    y_copy.start()
    send_cells(z % 4 >= 2)
    y_copy.wait()
    row_of = lax.broadcasted_iota(jnp.int32, (32, 512), 0)
    keep = row_of < 30
    for k in range(2):
        cells = jnp.where(keep, ybuf[k], 0.0)
        norms = jnp.sum(cells * cells, axis=0, keepdims=True)
        for q in range(4):
            flat = jnp.broadcast_to(norms[:, LANES * q : LANES * (q + 1)], (LANES, LANES))
            first = 512 * k + LANES * q
            vb[first : first + LANES, :] = jnp.transpose(flat)
        high, mid, low = three_parts(-2.0 * cells)
        stack = jnp.concatenate([jnp.where(row_of == 30, norms, high), mid, low, high], axis=0)
        yt[512 * k : 512 * (k + 1), :] = jnp.transpose(stack)
    for sub in range(8):
        turned = jnp.transpose(yt[pl.ds(sub, LANES, stride=8), :])
        yk[:, LANES * sub : LANES * (sub + 1)] = turned.astype(BF16)
        ysq[sub : sub + 1, :] = turned[30:31, :]

    def merge(first, second):
        peak = jnp.maximum(first[0], second[0])
        return peak, first[1] * jnp.exp2(first[0] - peak) + second[1] * jnp.exp2(second[0] - peak)

    columns = None
    for r in range(2):
        x_rows = []
        g_rows = []
        for k in range(2 * r, 2 * r + 2):
            block = xbuf.at[k]
            pltpu.make_async_copy(block, block, x_sem.at[k]).wait()
            cells = jnp.where(keep, xbuf[k], 0.0)
            norms = jnp.sum(cells * cells, axis=0, keepdims=True)
            x_rows += [norms[:, LANES * q : LANES * (q + 1)] for q in range(4)]
            g_rows += [xbuf[k, 30:31, LANES * q : LANES * (q + 1)] for q in range(4)]
            high, mid, low = three_parts(cells)
            none = jnp.zeros_like(high)
            for part, stack in enumerate(([high, high, high, none], [mid, mid, none, low])):
                stack = jnp.concatenate(stack, axis=0)
                xk[LANES * part : LANES * (part + 1), 512 * k : 512 * (k + 1)] = stack.astype(BF16)
                turned = jnp.transpose(stack)
                for q in range(4):
                    first = 1024 * r + 4 * (k % 2) + q
                    (xt0, xt1)[part][pl.ds(first, LANES, stride=8), :] = turned[LANES * q : LANES * (q + 1), :]
        grown = jnp.concatenate(g_rows, axis=0)
        log_a = jnp.where(row_ids[r] < live_now, jnp.log2(grown) - log_now, NEG)
        la[r] = log_a
        spread_columns(jnp.concatenate(x_rows, axis=0), ub.at[r])

        def ct_rows(k, carry, r=r, x_rows=x_rows):
            row = pl.multiple_of(k * 256, 256)
            left = yt[pl.ds(row, 256), :].astype(BF16)
            left = jnp.concatenate([left, left], axis=1)
            cross = jnp.dot(left, xk[:, 1024 * r : 1024 * (r + 1)], preferred_element_type=F32)
            for q in range(8):
                norm = vb[pl.ds(row, 256), :] + x_rows[q]
                ct[r, pl.ds(row, 256), LANES * q : LANES * (q + 1)] = (
                    norm + cross[:, LANES * q : LANES * (q + 1)]
                ) * COST_SCALE
            return carry

        lax.fori_loop(0, 4, ct_rows, 0)

        def cr_rows(k, carry, r=r):
            row = pl.multiple_of(k * 256, 256)
            both = pl.multiple_of(1024 * r + k * 256, 256)
            left = jnp.concatenate([xt0[pl.ds(both, 256), :], xt1[pl.ds(both, 256), :]], axis=1).astype(BF16)
            right = yk[...]
            cross = jnp.dot(left, jnp.concatenate([right, right], axis=0), preferred_element_type=F32)
            for q in range(8):
                norm = ub[r, pl.ds(row, 256), :] + ysq[q : q + 1, :]
                cr[r, pl.ds(row, 256), LANES * q : LANES * (q + 1)] = (
                    norm + cross[:, LANES * q : LANES * (q + 1)]
                ) * COST_SCALE
            return carry

        lax.fori_loop(0, 4, cr_rows, 0)
        spread_columns(log_a, ub.at[r])
        found = lse_pass(cr.at[r], ub.at[r])
        columns = found if columns is None else merge(columns, found)

    def from_columns(par, m0, s0):
        csend[par, 0:8] = m0
        csend[par, 8:16] = s0
        copy = push(csend.at[par], cslot.at[par], cs_send.at[par], cs_recv.at[par], at(*core_peer))
        copy.start()
        copy.wait()
        peak, total = merge((m0, s0), (cslot[par, 0:8], cslot[par, 8:16]))
        spread_columns(-SHRINK * (peak + jnp.log2(total)) + log_b, vb)

    def send_rows(par):
        def half(r, carry):
            m, s = lse_pass(ct.at[r], vb)
            rsend[par, r, 0:8] = m
            rsend[par, r, 8:16] = s
            rslot[par, r, b, 0:8] = m
            rslot[par, r, b, 8:16] = s
            for where in row_peers:
                push(
                    rsend.at[par, r], rslot.at[par, r, b], rs_send.at[par, r], rs_recv.at[par, r], at(*where)
                ).start()
            return carry

        lax.fori_loop(0, 2, half, 0)

    def from_rows(par, r):
        three = rslot.at[par, r, pl.ds(0, 3)]
        pltpu.make_async_copy(three, three, rs_recv.at[par, r]).wait()
        pltpu.make_async_copy(three, three, rs_send.at[par, r]).wait()
        ms = [rslot[par, r, k, 0:8] for k in range(4)]
        ss = [rslot[par, r, k, 8:16] for k in range(4)]
        peak = jnp.maximum(jnp.maximum(ms[0], ms[1]), jnp.maximum(ms[2], ms[3]))
        terms = [ss[k] * jnp.exp2(ms[k] - peak) for k in range(4)]
        total = (terms[0] + terms[1]) + (terms[2] + terms[3])
        return peak, total, -SHRINK * (peak + jnp.log2(total))

    def iterate(step, carry):
        par = step % 2
        from_columns(par, *carry)
        send_rows(par)

        def half(r, so_far):
            level = from_rows(par, r)[2]
            spread_columns(level + la[r], ub.at[r])
            return merge(so_far, lse_pass(cr.at[r], ub.at[r]))

        return lax.fori_loop(0, 2, half, (jnp.full((8, LANES), LOWEST, F32), jnp.zeros((8, LANES), F32)))

    columns = lax.fori_loop(0, ITERS - 1, iterate, columns)
    par = (ITERS - 1) % 2
    from_columns(par, *columns)
    send_rows(par)

    for r in range(2):
        wpeak = [rsend[par, r, q : q + 1, :] for q in range(8)]

        def w_rows(k, carry, r=r, wpeak=wpeak):
            for j in range(4):
                row = pl.multiple_of(k * 64 + 16 * j, 16)
                left = vb[pl.ds(row, 16), :]
                for q in range(8):
                    s = left - ct[r, pl.ds(row, 16), LANES * q : LANES * (q + 1)]
                    cr[r, pl.ds(row, 16), LANES * q : LANES * (q + 1)] = jnp.exp2(s - wpeak[q])
            return carry

        lax.fori_loop(0, QUARTER // 64, w_rows, 0)

    for r in range(2):
        peak, total, level = from_rows(par, r)
        fsend[8 * r : 8 * r + 8] = level * (EPS / LOG2E)
        scale = jnp.exp2(rsend[par, r, 0:8] - peak) / total
        scale = jnp.where(row_ids[r] < live_now, scale, 0.0)
        scales = [scale[q : q + 1, :] for q in range(8)]

        def round_rows(k, carry, r=r, scales=scales):
            for j in range(4):
                row = pl.multiple_of(k * 64 + 16 * j, 16)
                for q in range(8):
                    first = 1024 * r + LANES * q
                    w = cr[r, pl.ds(row, 16), LANES * q : LANES * (q + 1)] * scales[q]
                    wt[pl.ds(row, 16), first : first + LANES] = w.astype(BF16)
            return carry

        lax.fori_loop(0, QUARTER // 64, round_rows, 0)


    pot_copy = push(fsend, fother, p_send, p_recv, at(*core_peer))
    pot_copy.start()

    @pl.when(last)
    def _():
        pltpu.make_async_copy(hand, hand, f_sem).wait()

    @pl.when(jnp.logical_not(last))
    def _():
        pltpu.make_async_copy(chin, chin, ch_recv).wait()
        total = (chin[0] + chin[1]) + (chin[2] + chin[3])
        none = jnp.zeros((6, LANES), F32)
        for q in range(4):
            most = total[:, LANES * q : LANES * (q + 1)]
            tile = jnp.concatenate([most, total[2 * q : 2 * q + 2, 512:640], none], axis=0)
            hand[c, :, LANES * q : LANES * (q + 1)] = tile.astype(BF16)
        copy = push(hand.at[c], hand.at[c], hx_send, hx_recv, at(*core_peer))
        copy.start()
        copy.wait()

    handed = jnp.concatenate([hand[0], hand[1]], axis=1)
    for r in range(2):
        tiles = []
        part = jnp.dot(handed, wt[:, 1024 * r : 1024 * (r + 1)], preferred_element_type=F32)
        for q in range(8):
            tile = part[:, LANES * q : LANES * (q + 1)]
            pbuf[8 * r + q] = tile.astype(BF16)
            tiles.append(tile)
        for h in range(2):
            for q in range(4):
                pbf[r, h, :, LANES * q : LANES * (q + 1)] = tiles[4 * h + q][0:8]
            pbf[r, h, :, 512:640] = jnp.concatenate([tiles[4 * h + q][8:10] for q in range(4)], axis=0)
    for k, (cond, where) in enumerate(ch_to):
        @pl.when(cond)
        def _(k=k, where=where):
            push(pbf.at[k // 2, k % 2], chin.at[b], ch_send, ch_recv, at(*where)).start()

    @pl.when(c == home)
    def _():
        def send_out(k, carry):
            where = out_to(k)
            tile = pbuf.at[8 * (a % 2) + k // 4]
            mine = same(*where)

            @pl.when(jnp.logical_not(mine))
            def _():
                push(tile, s2.at[d, b], s2_send, s2_recv, at(*where)).start()

            @pl.when(mine)
            def _():
                pltpu.make_async_copy(tile, s2.at[d, b], s2_recv).start()

            return carry

        lax.fori_loop(0, 32, send_out, 0)

    pot_copy.wait()
    own = jnp.where(c == home, fsend[...], fother[...])
    picked = own[0:4]
    for k in range(1, 4):
        picked = jnp.where(z % 4 == k, own[4 * k : 4 * k + 4], picked)
    for k in range(4):
        pot_ref[0:1, LANES * k : LANES * (k + 1)] = picked[k : k + 1]

    pltpu.make_async_copy(s2, s2, s2_recv).wait()
    turn = lax.rem(LANES - 32 * quad, LANES)
    for g in range(4):
        four = [s2[g, k].astype(F32) for k in range(4)]
        tile = (four[0] + four[1]) + (four[2] + four[3])
        out_ref[0, 10 * g : 10 * g + 10, :] = pltpu.roll(tile, turn, axis=1)[0:10, 0:32]

    def settle(cond, ref, sem):
        @pl.when(cond)
        def _():
            pltpu.make_async_copy(ref, ref, sem).wait()

    for cond, where in x_to:
        settle(cond, xst, in_send)
    for cond, where in y_to:
        settle(cond, fst, in_send)
    for where in f_to:
        off = f_active & jnp.logical_not(same(*where))
        settle(off & (where[3] == c), fst, fs_send)
        settle(off, fates_st.at[0], fs_send)
    for cond, where in ch_to:
        settle(cond, pbf.at[0, 0], ch_send)
    settle(c == home, pbuf, s2_send)
    settle(c == home, pbuf.at[pl.ds(0, 15)], s2_send)


def local(src_cells, final_cells, growth, live, final_fates):
    vmem = pl.BlockSpec(memory_space=pltpu.VMEM)
    dma = pltpu.SemaphoreType.DMA
    V = pltpu.VMEM
    return tuple(pl.pallas_call(
        kernel,
        out_shape=(
            jax.ShapeDtypeStruct((1, 40, 32), F32),
            jax.ShapeDtypeStruct((1, 512), F32),
        ),
        in_specs=[vmem, vmem, vmem, pl.BlockSpec(memory_space=pltpu.SMEM), vmem],
        out_specs=(vmem, vmem),
        scratch_shapes=[
            V((32, 512), F32), V((32, 256), F32), V((4, 16, 256), BF16),
            V((4, 32, 512), F32), V((2, 32, 512), F32),
            V((256, HALF), BF16), V((HALF, 128), F32), V((HALF, 128), F32), V((QUARTER, 128), F32), V((128, QUARTER), BF16),
            V((8, 128), F32), V((2, 8, 128), F32),
            V((2, QUARTER, QUARTER), F32), V((2, QUARTER, QUARTER), F32),
            V((2, QUARTER, 128), F32), V((QUARTER, 128), F32), V((QUARTER, HALF), BF16),
            V((2, 16, 128), F32), V((2, 16, 128), F32), V((2, 2, 16, 128), F32), V((2, 2, 4, 16, 128), F32),
            V((16, 128), F32), V((16, 128), F32),
            V((2, 16, 512), BF16), V((16, 16, 128), BF16), V((2, 2, 8, 640), F32), V((4, 8, 640), F32),
            V((4, 4, 16, 128), BF16),
            dma(()), dma((4,)), dma(()), dma(()), dma(()), dma((2,)), dma((2,)), dma((2, 2)), dma((2, 2)),
            dma(()), dma(()), dma(()), dma(()), dma(()), dma(()), dma(()), dma(()), dma(()), dma(()),
        ],
        compiler_params=pltpu.CompilerParams(
            collective_id=0, has_side_effects=True, vmem_limit_bytes=48 * 2**20
        ),
        name="transport",
    )(jnp.transpose(src_cells, (1, 0, 2)), final_cells, growth, live, final_fates))


def solution(mesh):
    placed = (P("pair", None, "src"), P(None, "tgt"), P("pair", "src"), P(), P(None, "tgt"))
    return jax.shard_map(
        local,
        mesh=mesh,
        in_specs=placed,
        out_specs=(P("pair", None, ("src", "tgt")), P("pair", "src")),
        check_vma=False,
    )
```

```python
import functools
import math

import jax
import jax.numpy as jnp
from jax import lax
from jax.experimental import pallas as pl
from jax.experimental.pallas import tpu as pltpu
from jax.sharding import PartitionSpec as P

MESH = pl.DeviceIdType.MESH
F32 = jnp.float32
BF16 = jnp.bfloat16

ITERS = 8
EPS = 0.1
LAM = 1.0
NEG = -1e30
SHRINK = LAM / (LAM + EPS)
LOG2E = 1.0 / math.log(2.0)
COST_SCALE = LOG2E / (EPS * 60.0)
LOWEST = -3e38

HALF = 2048
QUARTER = 1024
LANES = 128
GROUP = 64


def lane_iota():
    return lax.broadcasted_iota(jnp.int32, (8, LANES), 1)


def sub_iota():
    return lax.broadcasted_iota(jnp.int32, (8, LANES), 0)


def spread_columns(packed, dst):
    for t in range(LANES):
        dst[8 * t : 8 * t + 8, :] = jnp.broadcast_to(packed[:, t : t + 1], (8, LANES))


def lse_pass(cost, spread):
    tiles = 8
    rows = 8 * GROUP

    def walk(start, update):
        def body(k, acc):
            acc = list(acc)
            first = pl.multiple_of(k * rows, rows)
            left_rows = spread.at[pl.ds(first, rows)]
            cost_rows = cost.at[pl.ds(first, rows)]
            for t in range(GROUP):
                left = left_rows[8 * t : 8 * t + 8, :]
                for q in range(tiles):
                    acc[q] = update(q, acc[q], left - cost_rows[8 * t : 8 * t + 8, LANES * q : LANES * (q + 1)])
            return tuple(acc)

        return lax.fori_loop(0, QUARTER // rows, body, tuple(start))

    peaks = walk([jnp.full((8, LANES), LOWEST, F32)] * tiles, lambda q, a, s: jnp.maximum(a, s))
    peaks = [jnp.broadcast_to(jnp.max(a, axis=0, keepdims=True), (8, LANES)) for a in peaks]
    sums = walk([jnp.zeros((8, LANES), F32)] * tiles, lambda q, a, s: a + jnp.exp2(s - peaks[q]))
    sums = [jnp.broadcast_to(jnp.sum(a, axis=0, keepdims=True), (8, LANES)) for a in sums]
    which = sub_iota()
    m, s = peaks[0], sums[0]
    for q in range(1, 8):
        m = jnp.where(which == q, peaks[q], m)
        s = jnp.where(which == q, sums[q], s)
    return m, s


def three_parts(x):
    high = x.astype(BF16).astype(F32)
    rest = x - high
    mid = rest.astype(BF16).astype(F32)
    low = (rest - mid).astype(BF16).astype(F32)
    return high, mid, low


def kernel(
    src_ref, fin_ref, growth_ref, live_ref, fates_ref, out_ref, pot_ref,
    xst, fst, fates_st, xbuf, ybuf, xk, xt0, xt1, yt, yk, ysq, la, ct, cr, ub, vb, wt,
    csend, cslot, rsend, rslot, fsend, fother, hand, pbuf, pbf, chin, s2,
    in_send, x_sem, y_sem, f_sem, fs_send, cs_send, cs_recv, rs_send, rs_recv,
    p_send, p_recv, ch_send, ch_recv, yf_send, yf_recv, s2_send, s2_recv, hx_send, hx_recv,
):
    p = lax.axis_index("pair")
    z = lax.axis_index("src")
    t = lax.axis_index("tgt")
    y, c = t // 2, t % 2
    zb, yb = z % 2, y % 2
    b = 2 * zb + yb
    z0, y0 = z - zb, y - yb
    a, d = z // 2, y // 2
    home = z // 4
    last = p == 3

    def at(pp, zz, yy, cc):
        return {"pair": pp, "src": zz, "tgt": 2 * yy + cc}

    def push(src, dst, send, recv, where):
        return pltpu.make_async_remote_copy(src, dst, send, recv, device_id=where, device_id_type=MESH)

    def same(pp, zz, yy, cc):
        return (pp == p) & (zz == z) & (yy == y) & (cc == c)

    up, down = jnp.minimum(p + 1, 3), jnp.maximum(p - 1, 0)
    chips = [3 - b, (b + 2) % 4, b + 1 - 2 * (b % 2)]
    chip_at = lambda bb: (z0 + bb // 2, y0 + bb % 2)
    core_peer = (p, z, y, 1 - c)
    row_peers = [(p, *chip_at(bb), c) for bb in chips]
    x_to = [(c == home, (p, (z + k) % 8, y, c)) for k in (4, 3, 5, 2, 6, 1, 7)]
    x_from = [(4 * c + k != z, (p, 4 * c + k, y, c)) for k in range(4)]
    y_active = (p > 0) & (yb == a % 2)
    y_to = [(y_active, (down, home + 2 * k, y, c)) for k in range(4)]
    y_from = [(p < 3, (up, 2 * b + k, y, c)) for k in range(2)]
    f_active = last & (zb == y // 4)
    f_to = [(p, z, d % 2 + 2 * (k // 2), k % 2) for k in range(8)]
    f_from = [(p, z, 2 * b + k // 2, k % 2) for k in range(4)]
    ch_to = [(p > 0, (down, *chip_at(2 * c + k // 2), k % 2)) for k in range(4)]
    ch_from = [(p < 3, (up, *chip_at(k), b // 2)) for k in range(4)]
    quad = 2 * yb + c

    def out_to(k):
        return p, z0 + k // 16, 2 * (k // 4 % 4) + k // 2 % 2, k % 2

    def out_from(k):
        return p, z0 + k // 8, 2 * (k // 2 % 4) + k % 2, home

    barrier = pltpu.get_barrier_semaphore()
    expected = jnp.int32(4)

    def greet(cond, where):
        @pl.when(cond)
        def _():
            pl.semaphore_signal(barrier, inc=1, device_id=at(*where), device_id_type=MESH)

    pl.semaphore_signal(barrier, inc=1, device_id=at(*core_peer), device_id_type=MESH)
    for where in row_peers:
        pl.semaphore_signal(barrier, inc=1, device_id=at(*where), device_id_type=MESH)
    for cond, where in x_from + y_from + ch_from:
        greet(cond, where)
    for where in f_from:
        greet(last & jnp.logical_not(same(*where)), where)
    for k in range(16):
        greet(jnp.logical_not(same(*out_from(k))), out_from(k))
    for cond, where in x_to + y_to + ch_to:
        expected = expected + jnp.where(cond, 1, 0)
    for where in f_to:
        expected = expected + jnp.where(f_active & jnp.logical_not(same(*where)), 1, 0)
    expected = expected + jnp.where(c == home, 31, 0)

    xst[30:32, :] = jnp.zeros((2, 512), F32)
    xst[0:30, :] = src_ref[:, 0, :]
    xst[30:31, :] = growth_ref[...]
    fst[...] = jnp.zeros_like(fst)
    fst[0:30, :] = fin_ref[...]
    for g in range(4):
        block = jnp.concatenate([fates_ref[10 * g : 10 * g + 10, :], jnp.zeros((6, 256), F32)], axis=0)
        fates_st[g] = block.astype(BF16)

    pl.semaphore_wait(barrier, expected)

    def my_lanes(ref):
        first = pl.multiple_of(256 * c, 256)
        return ref.at[:, pl.ds(first, 256)]

    for cond, where in y_to:
        @pl.when(cond)
        def _(where=where):
            push(my_lanes(xst), my_lanes(ybuf.at[zb]), in_send, y_sem, at(*where)).start()

    slot = t % 4
    fin_dst = ybuf.at[slot // 2, :, pl.ds(pl.multiple_of((slot % 2) * 256, 256), 256)]
    fate_dst = hand.at[slot // 2, :, pl.ds(pl.multiple_of((slot % 2) * 256, 256), 256)]
    for where in f_to:
        mine = same(*where)

        @pl.when(f_active & jnp.logical_not(mine) & (where[3] == c))
        def _(where=where):
            push(fst, fin_dst, fs_send, y_sem, at(*where)).start()

        @pl.when(f_active & jnp.logical_not(mine))
        def _(where=where):
            push(fates_st.at[where[2] // 2], fate_dst, fs_send, f_sem, at(*where)).start()

        @pl.when(f_active & mine)
        def _(where=where):
            pltpu.make_async_copy(fst, fin_dst, y_sem).start()
            pltpu.make_async_copy(fates_st.at[where[2] // 2], fate_dst, f_sem).start()

    def send_cells(chosen):
        for cond, where in x_to:
            @pl.when(cond & chosen)
            def _(where=where):
                push(xst, xbuf.at[z % 4], in_send, x_sem.at[z % 4], at(*where)).start()

        @pl.when((c == home) & chosen)
        def _():
            pltpu.make_async_copy(xst, xbuf.at[z % 4], x_sem.at[z % 4]).start()

    send_cells(z % 4 < 2)

    live_now = jnp.int32(0)
    live_next = jnp.int32(0)
    for k in range(4):
        live_now = live_now + jnp.where(p == k, live_ref[k], 0)
        live_next = live_next + jnp.where(p == k, live_ref[k + 1], 0)
    log_now = jnp.log2(jnp.broadcast_to(live_now.astype(F32), (8, LANES)))
    log_next = jnp.log2(jnp.broadcast_to(live_next.astype(F32), (8, LANES)))
    lanes, subs = lane_iota(), sub_iota()
    row_ids = [HALF * c + LANES * (8 * r + subs) + lanes for r in range(2)]
    col_ids = QUARTER * b + 8 * lanes + subs
    log_b = jnp.where(col_ids < live_next, -log_next, NEG)

    half = ybuf.at[:, :, pl.ds(0, 256)]
    pltpu.make_async_copy(half, half, y_sem).wait()
    mine = ybuf.at[:, :, pl.ds(pl.multiple_of(256 * c, 256), 256)]
    y_copy = push(mine, mine, yf_send, yf_recv, at(*core_peer))
    y_copy.start()
    send_cells(z % 4 >= 2)
    y_copy.wait()
    row_of = lax.broadcasted_iota(jnp.int32, (32, 512), 0)
    keep = row_of < 30
    for k in range(2):
        cells = jnp.where(keep, ybuf[k], 0.0)
        norms = jnp.sum(cells * cells, axis=0, keepdims=True)
        for q in range(4):
            flat = jnp.broadcast_to(norms[:, LANES * q : LANES * (q + 1)], (LANES, LANES))
            first = 512 * k + LANES * q
            vb[first : first + LANES, :] = jnp.transpose(flat)
        high, mid, low = three_parts(-2.0 * cells)
        stack = jnp.concatenate([jnp.where(row_of == 30, norms, high), mid, low, high], axis=0)
        yt[512 * k : 512 * (k + 1), :] = jnp.transpose(stack)
    for sub in range(8):
        turned = jnp.transpose(yt[pl.ds(sub, LANES, stride=8), :])
        yk[:, LANES * sub : LANES * (sub + 1)] = turned.astype(BF16)
        ysq[sub : sub + 1, :] = turned[30:31, :]

    def merge(first, second):
        peak = jnp.maximum(first[0], second[0])
        return peak, first[1] * jnp.exp2(first[0] - peak) + second[1] * jnp.exp2(second[0] - peak)

    columns = None
    for r in range(2):
        x_rows = []
        g_rows = []
        for k in range(2 * r, 2 * r + 2):
            block = xbuf.at[k]
            pltpu.make_async_copy(block, block, x_sem.at[k]).wait()
            cells = jnp.where(keep, xbuf[k], 0.0)
            norms = jnp.sum(cells * cells, axis=0, keepdims=True)
            x_rows += [norms[:, LANES * q : LANES * (q + 1)] for q in range(4)]
            g_rows += [xbuf[k, 30:31, LANES * q : LANES * (q + 1)] for q in range(4)]
            high, mid, low = three_parts(cells)
            none = jnp.zeros_like(high)
            for part, stack in enumerate(([high, high, high, none], [mid, mid, none, low])):
                stack = jnp.concatenate(stack, axis=0)
                xk[LANES * part : LANES * (part + 1), 512 * k : 512 * (k + 1)] = stack.astype(BF16)
                turned = jnp.transpose(stack)
                for q in range(4):
                    first = 1024 * r + 4 * (k % 2) + q
                    (xt0, xt1)[part][pl.ds(first, LANES, stride=8), :] = turned[LANES * q : LANES * (q + 1), :]
        grown = jnp.concatenate(g_rows, axis=0)
        log_a = jnp.where(row_ids[r] < live_now, jnp.log2(grown) - log_now, NEG)
        la[r] = log_a
        spread_columns(jnp.concatenate(x_rows, axis=0), ub.at[r])

        def ct_rows(k, carry, r=r, x_rows=x_rows):
            row = pl.multiple_of(k * 256, 256)
            left = yt[pl.ds(row, 256), :].astype(BF16)
            left = jnp.concatenate([left, left], axis=1)
            cross = jnp.dot(left, xk[:, 1024 * r : 1024 * (r + 1)], preferred_element_type=F32)
            for q in range(8):
                norm = vb[pl.ds(row, 256), :] + x_rows[q]
                ct[r, pl.ds(row, 256), LANES * q : LANES * (q + 1)] = (
                    norm + cross[:, LANES * q : LANES * (q + 1)]
                ) * COST_SCALE
            return carry

        lax.fori_loop(0, 4, ct_rows, 0)

        def cr_rows(k, carry, r=r):
            row = pl.multiple_of(k * 256, 256)
            both = pl.multiple_of(1024 * r + k * 256, 256)
            left = jnp.concatenate([xt0[pl.ds(both, 256), :], xt1[pl.ds(both, 256), :]], axis=1).astype(BF16)
            right = yk[...]
            cross = jnp.dot(left, jnp.concatenate([right, right], axis=0), preferred_element_type=F32)
            for q in range(8):
                norm = ub[r, pl.ds(row, 256), :] + ysq[q : q + 1, :]
                cr[r, pl.ds(row, 256), LANES * q : LANES * (q + 1)] = (
                    norm + cross[:, LANES * q : LANES * (q + 1)]
                ) * COST_SCALE
            return carry

        lax.fori_loop(0, 4, cr_rows, 0)
        spread_columns(log_a, ub.at[r])
        found = lse_pass(cr.at[r], ub.at[r])
        columns = found if columns is None else merge(columns, found)

    def from_columns(par, m0, s0):
        csend[par, 0:8] = m0
        csend[par, 8:16] = s0
        copy = push(csend.at[par], cslot.at[par], cs_send.at[par], cs_recv.at[par], at(*core_peer))
        copy.start()
        copy.wait()
        peak, total = merge((m0, s0), (cslot[par, 0:8], cslot[par, 8:16]))
        spread_columns(-SHRINK * (peak + jnp.log2(total)) + log_b, vb)

    def send_rows(par):
        def half(r, carry):
            m, s = lse_pass(ct.at[r], vb)
            rsend[par, r, 0:8] = m
            rsend[par, r, 8:16] = s
            rslot[par, r, b, 0:8] = m
            rslot[par, r, b, 8:16] = s
            for where in row_peers:
                push(
                    rsend.at[par, r], rslot.at[par, r, b], rs_send.at[par, r], rs_recv.at[par, r], at(*where)
                ).start()
            return carry

        lax.fori_loop(0, 2, half, 0)

    def from_rows(par, r):
        three = rslot.at[par, r, pl.ds(0, 3)]
        pltpu.make_async_copy(three, three, rs_recv.at[par, r]).wait()
        pltpu.make_async_copy(three, three, rs_send.at[par, r]).wait()
        ms = [rslot[par, r, k, 0:8] for k in range(4)]
        ss = [rslot[par, r, k, 8:16] for k in range(4)]
        peak = jnp.maximum(jnp.maximum(ms[0], ms[1]), jnp.maximum(ms[2], ms[3]))
        terms = [ss[k] * jnp.exp2(ms[k] - peak) for k in range(4)]
        total = (terms[0] + terms[1]) + (terms[2] + terms[3])
        return peak, total, -SHRINK * (peak + jnp.log2(total))

    def iterate(step, carry):
        par = step % 2
        from_columns(par, *carry)
        send_rows(par)

        def half(r, so_far):
            level = from_rows(par, r)[2]
            spread_columns(level + la[r], ub.at[r])
            return merge(so_far, lse_pass(cr.at[r], ub.at[r]))

        return lax.fori_loop(0, 2, half, (jnp.full((8, LANES), LOWEST, F32), jnp.zeros((8, LANES), F32)))

    columns = lax.fori_loop(0, ITERS - 1, iterate, columns)
    par = (ITERS - 1) % 2
    from_columns(par, *columns)
    send_rows(par)

    for r in range(2):
        wpeak = [rsend[par, r, q : q + 1, :] for q in range(8)]

        def w_rows(k, carry, r=r, wpeak=wpeak):
            for j in range(4):
                row = pl.multiple_of(k * 64 + 16 * j, 16)
                left = vb[pl.ds(row, 16), :]
                for q in range(8):
                    s = left - ct[r, pl.ds(row, 16), LANES * q : LANES * (q + 1)]
                    cr[r, pl.ds(row, 16), LANES * q : LANES * (q + 1)] = jnp.exp2(s - wpeak[q])
            return carry

        lax.fori_loop(0, QUARTER // 64, w_rows, 0)

    for r in range(2):
        peak, total, level = from_rows(par, r)
        fsend[8 * r : 8 * r + 8] = level * (EPS / LOG2E)
        scale = jnp.exp2(rsend[par, r, 0:8] - peak) / total
        scale = jnp.where(row_ids[r] < live_now, scale, 0.0)
        scales = [scale[q : q + 1, :] for q in range(8)]

        def round_rows(k, carry, r=r, scales=scales):
            for j in range(4):
                row = pl.multiple_of(k * 64 + 16 * j, 16)
                for q in range(8):
                    first = 1024 * r + LANES * q
                    w = cr[r, pl.ds(row, 16), LANES * q : LANES * (q + 1)] * scales[q]
                    wt[pl.ds(row, 16), first : first + LANES] = w.astype(BF16)
            return carry

        lax.fori_loop(0, QUARTER // 64, round_rows, 0)


    pot_copy = push(fsend, fother, p_send, p_recv, at(*core_peer))
    pot_copy.start()

    @pl.when(last)
    def _():
        pltpu.make_async_copy(hand, hand, f_sem).wait()

    @pl.when(jnp.logical_not(last))
    def _():
        pltpu.make_async_copy(chin, chin, ch_recv).wait()
        total = (chin[0] + chin[1]) + (chin[2] + chin[3])
        none = jnp.zeros((6, LANES), F32)
        for q in range(4):
            most = total[:, LANES * q : LANES * (q + 1)]
            tile = jnp.concatenate([most, total[2 * q : 2 * q + 2, 512:640], none], axis=0)
            hand[c, :, LANES * q : LANES * (q + 1)] = tile.astype(BF16)
        copy = push(hand.at[c], hand.at[c], hx_send, hx_recv, at(*core_peer))
        copy.start()
        copy.wait()

    handed = jnp.concatenate([hand[0], hand[1]], axis=1)
    for r in range(2):
        tiles = []
        part = jnp.dot(handed, wt[:, 1024 * r : 1024 * (r + 1)], preferred_element_type=F32)
        for q in range(8):
            tile = part[:, LANES * q : LANES * (q + 1)]
            pbuf[8 * r + q] = tile.astype(BF16)
            tiles.append(tile)
        for h in range(2):
            for q in range(4):
                pbf[r, h, :, LANES * q : LANES * (q + 1)] = tiles[4 * h + q][0:8]
            pbf[r, h, :, 512:640] = jnp.concatenate([tiles[4 * h + q][8:10] for q in range(4)], axis=0)
            cond, where = ch_to[2 * r + h]

            @pl.when(cond)
            def _(r=r, h=h, where=where):
                push(pbf.at[r, h], chin.at[b], ch_send, ch_recv, at(*where)).start()

    @pl.when(c == home)
    def _():
        def send_out(k, carry):
            where = out_to(k)
            tile = pbuf.at[8 * (a % 2) + k // 4]
            mine = same(*where)

            @pl.when(jnp.logical_not(mine))
            def _():
                push(tile, s2.at[d, b], s2_send, s2_recv, at(*where)).start()

            @pl.when(mine)
            def _():
                pltpu.make_async_copy(tile, s2.at[d, b], s2_recv).start()

            return carry

        lax.fori_loop(0, 32, send_out, 0)

    pot_copy.wait()
    own = jnp.where(c == home, fsend[...], fother[...])
    picked = own[0:4]
    for k in range(1, 4):
        picked = jnp.where(z % 4 == k, own[4 * k : 4 * k + 4], picked)
    for k in range(4):
        pot_ref[0:1, LANES * k : LANES * (k + 1)] = picked[k : k + 1]

    pltpu.make_async_copy(s2, s2, s2_recv).wait()
    turn = lax.rem(LANES - 32 * quad, LANES)
    for g in range(4):
        four = [s2[g, k].astype(F32) for k in range(4)]
        tile = (four[0] + four[1]) + (four[2] + four[3])
        out_ref[0, 10 * g : 10 * g + 10, :] = pltpu.roll(tile, turn, axis=1)[0:10, 0:32]

    def settle(cond, ref, sem):
        @pl.when(cond)
        def _():
            pltpu.make_async_copy(ref, ref, sem).wait()

    for cond, where in x_to:
        settle(cond, xst, in_send)
    for cond, where in y_to:
        settle(cond, fst, in_send)
    for where in f_to:
        off = f_active & jnp.logical_not(same(*where))
        settle(off & (where[3] == c), fst, fs_send)
        settle(off, fates_st.at[0], fs_send)
    for cond, where in ch_to:
        settle(cond, pbf.at[0, 0], ch_send)
    settle(c == home, pbuf, s2_send)
    settle(c == home, pbuf.at[pl.ds(0, 15)], s2_send)


def local(src_cells, final_cells, growth, live, final_fates):
    vmem = pl.BlockSpec(memory_space=pltpu.VMEM)
    dma = pltpu.SemaphoreType.DMA
    V = pltpu.VMEM
    return tuple(pl.pallas_call(
        kernel,
        out_shape=(
            jax.ShapeDtypeStruct((1, 40, 32), F32),
            jax.ShapeDtypeStruct((1, 512), F32),
        ),
        in_specs=[vmem, vmem, vmem, pl.BlockSpec(memory_space=pltpu.SMEM), vmem],
        out_specs=(vmem, vmem),
        scratch_shapes=[
            V((32, 512), F32), V((32, 256), F32), V((4, 16, 256), BF16),
            V((4, 32, 512), F32), V((2, 32, 512), F32),
            V((256, HALF), BF16), V((HALF, 128), F32), V((HALF, 128), F32), V((QUARTER, 128), F32), V((128, QUARTER), BF16),
            V((8, 128), F32), V((2, 8, 128), F32),
            V((2, QUARTER, QUARTER), F32), V((2, QUARTER, QUARTER), F32),
            V((2, QUARTER, 128), F32), V((QUARTER, 128), F32), V((QUARTER, HALF), BF16),
            V((2, 16, 128), F32), V((2, 16, 128), F32), V((2, 2, 16, 128), F32), V((2, 2, 4, 16, 128), F32),
            V((16, 128), F32), V((16, 128), F32),
            V((2, 16, 512), BF16), V((16, 16, 128), BF16), V((2, 2, 8, 640), F32), V((4, 8, 640), F32),
            V((4, 4, 16, 128), BF16),
            dma(()), dma((4,)), dma(()), dma(()), dma(()), dma((2,)), dma((2,)), dma((2, 2)), dma((2, 2)),
            dma(()), dma(()), dma(()), dma(()), dma(()), dma(()), dma(()), dma(()), dma(()), dma(()),
        ],
        compiler_params=pltpu.CompilerParams(
            collective_id=0, has_side_effects=True, vmem_limit_bytes=48 * 2**20
        ),
        name="transport",
    )(jnp.transpose(src_cells, (1, 0, 2)), final_cells, growth, live, final_fates))


def solution(mesh):
    placed = (P("pair", None, "src"), P(None, "tgt"), P("pair", "src"), P(), P(None, "tgt"))
    return jax.shard_map(
        local,
        mesh=mesh,
        in_specs=placed,
        out_specs=(P("pair", None, ("src", "tgt")), P("pair", "src")),
        check_vma=False,
    )
```
